512 devices in a mesh: op: 16 (over y_hi, x, core), sec: 32 (over y_lo, z).
Axes of the slice: x: 4, y: 4 (y_hi: 2, y_lo: 2; y = y_hi * 2 + y_lo), z: 16, core: 2. Of those that a mesh axis runs over, the one named last changes fastest.
Arguments:
- start_vector: bfloat16 [64, 512, 512], P('sec'), may hold values from -100 to 100
- left_operators: bfloat16 [16, 64, 512, 512], P('op', 'sec'), may hold values from -0.25 to 0.25
- right_operators: bfloat16 [16, 64, 512, 512], P('op', 'sec'), may hold values from -0.25 to 0.25
- left_energy: float32 [64, 512], P('sec'), may hold values from -2 to 2
- right_energy: float32 [64, 512], P('sec'), may hold values from -2 to 2
- sector_size: int32 [64], replicated, may hold values from 64 to 512, as said below
- sector_spin: int32 [64], replicated, may hold values from 0 to 8
Outputs:
- ritz_vector: bfloat16 [64, 512, 512], P('sec', 'op')
- ritz_residual: bfloat16 [64, 512, 512], P('sec', 'op')
- energies: float32 [2], replicated
The draws below stay inside these ranges and needn't reach their ends.
Inputs may be any that keep to these rules, and one draw needn't show every extreme that they name: `sector_size`: at least one sector has exactly 512 states and one exactly 64.
All inputs are finite; a program needn't handle non-finite values.
Results may differ from the reference program's by a relative error of at most 0.033.
Values may be sent and summed in bfloat16 or wider, within the bound.
No kernel may reach another device: no remote copies, remote signals or barrier semaphores. Data moves between devices by JAX's collectives and lax.ppermute only.
A program may use at most 64 MiB of HBM per device.

```python
import math
import jax
import jax.numpy as jnp
from jax import lax

W = 512
NSEC = 64
NOPS = 16
N_OP = 16


def draw_start_vector(key, part):
    key = jax.random.fold_in(key, 5)
    base_key, row_key, column_key = jax.random.split(key, 3)
    base_values = jax.random.normal(base_key, (NSEC, W, W), jnp.float32)
    row_reach = math.log(10.0)
    row_scale = jnp.exp(jax.random.uniform(row_key, (NSEC, W, 1), jnp.float32, 0.0, row_reach))
    column_scale = jnp.exp(jax.random.uniform(column_key, (NSEC, 1, W), jnp.float32, 0.0, math.log(10.0)))
    return jnp.clip(0.1 * base_values * row_scale * column_scale, -100.0, 100.0).astype(jnp.bfloat16)


def skewed_levels(key, power):
    fraction = jax.random.uniform(key, (NSEC, W), jnp.float32, 0.0, 1.0)
    return jnp.clip(-2.0 + 4.0 * fraction ** power, -2.0, 2.0).astype(jnp.float32)


def draw_left_energy(key, part):
    key = jax.random.fold_in(key, 17)
    return skewed_levels(key, 3.0)


def draw_right_energy(key, part):
    key = jax.random.fold_in(key, 23)
    return skewed_levels(key, 3.0)


def draw_sector_size(key, part):
    key = jax.random.fold_in(key, 11)
    size_key, pick_key = jax.random.split(key)
    smallest = W // 8
    sizes = jax.random.randint(size_key, (NSEC,), smallest, W + 1)
    picks = jax.random.permutation(pick_key, NSEC)
    sizes = sizes.at[picks[0]].set(W)
    sizes = sizes.at[picks[1]].set(smallest)
    return sizes.astype(jnp.int32)


def touch_ends(array, key, low, high):
    index_at = [jax.random.randint(jax.random.fold_in(key, axis), (), 0, length) for axis, length in enumerate(array.shape)]
    main_axis = array.shape.index(max(array.shape))
    beside = index_at[:main_axis] + [(index_at[main_axis] + 1) % array.shape[main_axis]] + index_at[main_axis + 1:]
    return array.at[tuple(index_at)].set(low).at[tuple(beside)].set(high)


def shard_levels(stream_key, dims, cuts, low, high):
    factor_of, own = 1.0, jax.random.fold_in(stream_key, 6)
    for dim, blocks in cuts:
        draws = jnp.exp(jax.random.uniform(jax.random.fold_in(own, dim), (blocks,), jnp.float32, low / len(cuts), high / len(cuts)))
        factor_of = factor_of * jnp.repeat(draws, dims[dim] // blocks).reshape([-1 if axis == dim else 1 for axis in range(len(dims))])
    return factor_of


def centred(rng, shape, deviation, limit, shards=(), kind=jnp.bfloat16):
    level = shard_levels(rng, shape, shards, -0.22, 0.18) if shards else 1.0
    values = jax.random.normal(rng, shape, jnp.float32) * deviation * level
    return jnp.minimum(jnp.maximum(values, -limit), limit).astype(kind)


def setup_inputs(seed: int = 0) -> dict:
    streams_of = jax.random.split(jax.random.key(seed), 8)
    start_vector = draw_start_vector(jax.random.fold_in(streams_of[7], 71), 0)
    left_operators = centred(streams_of[1], (NOPS, NSEC, W, W), W ** -0.5, 0.25, ((0, 16), (1, 32)))
    right_operators = centred(streams_of[2], (NOPS, NSEC, W, W), W ** -0.5, 0.25, ((0, 16), (1, 32)))
    left_energy = draw_left_energy(jax.random.fold_in(streams_of[7], 71), 0)
    right_energy = draw_right_energy(jax.random.fold_in(streams_of[7], 71), 0)
    sector_size = draw_sector_size(jax.random.fold_in(streams_of[7], 71), 0)
    sector_spin = touch_ends(jax.random.randint(streams_of[6], (NSEC,), 0, 9), jax.random.fold_in(streams_of[6], 1), 0, 8).astype(jnp.int32)
    return dict(start_vector=start_vector, left_operators=left_operators, right_operators=right_operators, left_energy=left_energy, right_energy=right_energy, sector_size=sector_size, sector_spin=sector_spin)


precise = lax.Precision.HIGHEST

def sector_mask(sector_size):
    positions = jnp.arange(W, dtype=jnp.int32)
    inside = positions[None, :] < sector_size[:, None]
    return inside[:, :, None] & inside[:, None, :]

def sector_coupling(sector_spin):
    spins = sector_spin.astype(jnp.float32)
    ratio = jnp.sqrt((spins[1:] + 1.0) / (spins[:-1] + 1.0))
    return jnp.concatenate([ratio, jnp.zeros((1,), jnp.float32)])

def apply_operator(vector, left_operators, right_operators, coupling, cell_mask, diagonal):
    following = jnp.concatenate([vector[1:], jnp.zeros_like(vector[:1])], axis=0)
    per_index = NOPS // N_OP

    def sector_terms(carried, sector):
        left_block = lax.dynamic_index_in_dim(left_operators, sector, 1, keepdims=False).astype(jnp.float32)
        right_block = lax.dynamic_index_in_dim(right_operators, sector, 1, keepdims=False).astype(jnp.float32)
        source = lax.dynamic_index_in_dim(vector, sector, 0, keepdims=False).astype(jnp.float32)
        target = lax.dynamic_index_in_dim(following, sector, 0, keepdims=False).astype(jnp.float32)
        factor = lax.dynamic_index_in_dim(coupling, sector, 0, keepdims=False)
        right_image = jnp.einsum('ij,kqj->kiq', source, right_block, precision=precise).astype(jnp.bfloat16)
        right_image = lax.optimization_barrier(right_image).astype(jnp.float32)
        raised = factor * jnp.einsum('kpi,kiq->kpq', left_block, right_image, precision=precise)
        left_image = jnp.einsum('kpi,pj->kij', left_block, target, precision=precise).astype(jnp.bfloat16)
        left_image = lax.optimization_barrier(left_image).astype(jnp.float32)
        lowered = factor * jnp.einsum('kij,kjq->kiq', left_image, right_block, precision=precise)
        partial_value = (carried + lowered).reshape(N_OP, per_index, W, W).sum(axis=1)
        rounded = lax.optimization_barrier(partial_value.astype(jnp.bfloat16)).astype(jnp.float32)
        return (raised, rounded.sum(axis=0))
    sectors = jnp.arange(NSEC, dtype=jnp.int32)
    last_raised, summed = lax.scan(sector_terms, jnp.zeros((NOPS, W, W), jnp.float32), sectors)
    return jnp.where(cell_mask, summed + diagonal * vector.astype(jnp.float32), 0.0)

def reference(start_vector, left_operators, right_operators, left_energy, right_energy, sector_size, sector_spin):
    cell_mask = sector_mask(sector_size)
    coupling = sector_coupling(sector_spin)
    diagonal = left_energy[:, :, None] + right_energy[:, None, :]
    masked_start = jnp.where(cell_mask, start_vector, jnp.zeros_like(start_vector))
    first_image = apply_operator(masked_start, left_operators, right_operators, coupling, cell_mask, diagonal)
    start_values = masked_start.astype(jnp.float32)
    start_norm = jnp.sum(start_values * start_values)
    start_energy = jnp.sum(start_values * first_image)
    rayleigh = start_energy / start_norm
    start_scale = jnp.sqrt(start_norm)
    unit_start = start_values / start_scale
    unit_image = first_image / start_scale
    residual_first = unit_image - rayleigh * unit_start
    correction = residual_first / (jnp.abs(diagonal - rayleigh) + 1.0)
    correlation = jnp.sum(unit_start * correction)
    remainder = correction - correlation * unit_start
    spread = jnp.sum(remainder * remainder)
    unit_second = remainder / jnp.sqrt(spread)
    second_vector = unit_second.astype(jnp.bfloat16)
    second_image = apply_operator(second_vector, left_operators, right_operators, coupling, cell_mask, diagonal)
    cross_term = jnp.sum(unit_start * second_image)
    second_energy = jnp.sum(unit_second * second_image)
    half_gap = 0.5 * (rayleigh - second_energy)
    lowest = 0.5 * (rayleigh + second_energy) - jnp.sqrt(half_gap * half_gap + cross_term * cross_term)
    rotation = 0.5 * jnp.arctan2(2.0 * cross_term, rayleigh - second_energy)
    sine_angle = jnp.sin(rotation)
    cosine_angle = jnp.cos(rotation)
    ritz_unit = sine_angle * unit_start - cosine_angle * unit_second
    ritz_vector = (start_scale * ritz_unit).astype(jnp.bfloat16)
    ritz_residual = (start_scale * (sine_angle * unit_image - cosine_angle * second_image - lowest * ritz_unit)).astype(jnp.bfloat16)
    return (ritz_vector, ritz_residual, jnp.stack([rayleigh, lowest]))
```

```python
import functools

import jax
import jax.numpy as jnp
from jax import lax
from jax.experimental import pallas as pl
from jax.experimental.pallas import tpu as pltpu
from jax.sharding import Mesh, PartitionSpec as P

F32 = jnp.float32
BF16 = jnp.bfloat16
OP = ("yh", "x", "c")
CHIPS = ("yh", "x")
SEC = ("yl", "z")
WIDTH = 512
ROWS = 32
HALF = 256
NCHIP = 8
BLOCKS = 3
PART = BLOCKS * ROWS + 16
VMEM_LIMIT = 48 * 1024 * 1024


def call(kernel, out_shape, in_specs, scratch=(), flops=0, nbytes=1 << 20):
    return pl.pallas_call(
        kernel,
        out_shape=out_shape,
        in_specs=in_specs,
        out_specs=jax.tree.map(lambda _: pl.BlockSpec(memory_space=pltpu.VMEM), out_shape),
        scratch_shapes=list(scratch),
        compiler_params=pltpu.CompilerParams(vmem_limit_bytes=VMEM_LIMIT),
        cost_estimate=pl.CostEstimate(flops=flops, bytes_accessed=nbytes, transcendentals=0),
    )


VM = pl.BlockSpec(memory_space=pltpu.VMEM)
SM = pl.BlockSpec(memory_space=pltpu.SMEM)


def product(first, second, second_axis=0):
    return lax.dot_general(
        first, second, (((1,), (second_axis,)), ((), ())), preferred_element_type=F32
    )


def group(chip, core):
    return pl.multiple_of((2 * chip + core) * ROWS, ROWS)


def total(array):
    return jnp.sum(jnp.sum(array, axis=0, keepdims=True), axis=1, keepdims=True)


def lanes(values, width):
    place = lax.broadcasted_iota(jnp.int32, (1, width), 1)
    row = jnp.zeros((1, width), F32)
    for index, value in enumerate(values):
        row = jnp.where(place == index, value, row)
    return row


def sort_kernel(place_ref, left_ref, keep_ref, send_ref, turned):
    core = place_ref[0]
    for sector in range(2):
        turned[...] = left_ref[0, sector].T
        for chip in range(NCHIP):
            here = pl.ds(chip * ROWS, ROWS)
            keep_ref[sector, here] = left_ref[0, sector, pl.ds(group(chip, core), ROWS)]
            send_ref[sector, here] = left_ref[0, sector, pl.ds(group(chip, 1 - core), ROWS)]
            keep_ref[2 + sector, here] = turned[pl.ds(group(chip, core), ROWS)]
            send_ref[2 + sector, here] = turned[pl.ds(group(chip, 1 - core), ROWS)]


def image_blocks(place_ref, spin_ref, keep_ref, other_ref, right_ref, swapped_ref, field):
    first = place_ref[2]
    blocks = [None, None, None]
    for sector in range(2):
        here = first + sector
        following = jnp.minimum(here + 1, spin_ref.shape[0] - 1)
        above = jnp.full((1, WIDTH), spin_ref[following], jnp.int32).astype(F32) + 1.0
        below = jnp.full((1, WIDTH), spin_ref[here], jnp.int32).astype(F32) + 1.0
        linked = jnp.full((1, WIDTH), here, jnp.int32) + 1 < spin_ref.shape[0]
        coupling = jnp.where(linked, jnp.sqrt(above / below), 0.0)
        lowered = raised = None
        for left, right in ((keep_ref, right_ref.at[0]), (other_ref, swapped_ref.at[0])):
            left_image = product(left[2 + sector], field[sector + 1]).astype(BF16)
            down = product(left_image, right[sector])
            left_product = product(left[sector], field[sector]).astype(BF16)
            up = product(left_product, right[sector], 1)
            lowered = down if lowered is None else lowered + down
            raised = up if raised is None else raised + up
        lowered = coupling * lowered
        blocks[sector] = lowered if blocks[sector] is None else blocks[sector] + lowered
        blocks[sector + 1] = coupling * raised
    return blocks


def put_parts(place_ref, blocks, field, scalars, parts_ref):
    core = place_ref[0]
    energy = jnp.zeros((ROWS, WIDTH), F32)
    for index, block in enumerate(blocks):
        rounded = block.astype(BF16)
        for chip in range(NCHIP):
            piece = rounded[chip * ROWS : (chip + 1) * ROWS]
            parts_ref[chip, index * ROWS : (index + 1) * ROWS] = piece
            own = field[index, pl.ds(group(chip, core), ROWS)]
            energy = energy + piece.astype(F32) * own.astype(F32)
    row = lanes([total(energy)], WIDTH) + scalars
    high = row.astype(BF16)
    rest = row - high.astype(F32)
    middle = rest.astype(BF16)
    low = (rest - middle.astype(F32)).astype(BF16)
    place = lax.broadcasted_iota(jnp.int32, (16, WIDTH), 0)
    coded = jnp.where(
        place == 0,
        high.astype(F32),
        jnp.where(place == 1, middle.astype(F32), jnp.where(place == 2, low.astype(F32), 0.0)),
    ).astype(BF16)
    for chip in range(NCHIP):
        parts_ref[chip, BLOCKS * ROWS :] = coded


def inside(size, first_row, shape):
    rows = lax.broadcasted_iota(jnp.int32, shape, 0) + first_row
    columns = lax.broadcasted_iota(jnp.int32, shape, 1)
    return (rows < size) & (columns < size)


def size_of(place_ref, size_ref, block):
    return size_ref[jnp.minimum(place_ref[2] + block, size_ref.shape[0] - 1)]


def first_kernel(
    place_ref, size_ref, spin_ref, start_ref, halo_ref, diagonal_ref,
    keep_ref, other_ref, right_ref, swapped_ref, parts_ref, rows_ref, field,
):
    for block in range(BLOCKS):
        source = halo_ref[...] if block == 2 else start_ref[block]
        mask = inside(size_of(place_ref, size_ref, block), 0, (WIDTH, WIDTH))
        field[block] = jnp.where(mask, source.astype(F32), 0.0).astype(BF16)
    norm = jnp.zeros((ROWS, WIDTH), F32)
    energy = jnp.zeros((ROWS, WIDTH), F32)
    for block in range(BLOCKS):
        own = field[block, pl.ds(group(place_ref[1], place_ref[0]), ROWS)].astype(F32)
        rows_ref[block] = own
        if block < 2:
            norm = norm + own * own
            energy = energy + diagonal_ref[block] * (own * own)
    blocks = image_blocks(place_ref, spin_ref, keep_ref, other_ref, right_ref, swapped_ref, field)
    put_parts(place_ref, blocks, field, lanes([total(energy), total(norm)], WIDTH), parts_ref)


def second_kernel(
    place_ref, spin_ref, near_ref, far_ref, scalar_ref,
    keep_ref, other_ref, right_ref, swapped_ref, parts_ref, field,
):
    core = place_ref[0]
    for chip in range(NCHIP):
        for block in range(BLOCKS):
            there = pl.ds(block * ROWS, ROWS)
            field[block, pl.ds(group(chip, core), ROWS)] = near_ref[chip, there]
            field[block, pl.ds(group(chip, 1 - core), ROWS)] = far_ref[chip, there]
    blocks = image_blocks(place_ref, spin_ref, keep_ref, other_ref, right_ref, swapped_ref, field)
    put_parts(place_ref, blocks, field, scalar_ref[...], parts_ref)


def sum_kernel(received_ref, first_ref, second_ref, leaving_ref, scalar_ref):
    for index, out_ref in enumerate((first_ref, second_ref, leaving_ref)):
        running = jnp.zeros((ROWS, WIDTH), F32)
        for chip in range(NCHIP):
            running = running + received_ref[chip, index * ROWS : (index + 1) * ROWS].astype(F32)
        out_ref[...] = running
    coded = jnp.zeros((16, WIDTH), F32)
    for chip in range(NCHIP):
        coded = coded + received_ref[chip, BLOCKS * ROWS :].astype(F32)
    row = jnp.sum(coded, axis=0, keepdims=True)[:, :128]
    scalar_ref[...] = jnp.broadcast_to(row[None], scalar_ref.shape)


def scalars_of(gathered_ref, count):
    row = jnp.sum(jnp.sum(gathered_ref[...], axis=0), axis=0, keepdims=True) * (
        1.0 / gathered_ref.shape[1]
    )
    return [row[:, index : index + 1] for index in range(count)]


def correction_kernel(
    place_ref, size_ref, gathered_ref, first_ref, second_ref, leaving_ref, arrived_ref,
    ahead_ref, diagonal_ref, rows_ref, spread_ref, image_ref, change_ref, scalar_ref, known_ref,
):
    energy, norm = scalars_of(gathered_ref, 2)
    rayleigh = energy / norm
    scale = jnp.sqrt(norm)
    first_row = group(place_ref[1], place_ref[0])
    sums = [first_ref[...] + arrived_ref[...], second_ref[...], leaving_ref[...] + ahead_ref[...]]
    amounts = [jnp.zeros((ROWS, WIDTH), F32) for _ in range(4)]
    for block in range(BLOCKS):
        mask = inside(size_of(place_ref, size_ref, block), first_row, (ROWS, WIDTH))
        values = rows_ref[block]
        diagonal = diagonal_ref[block]
        unit = values / scale
        image = jnp.where(mask, sums[block] + diagonal * values, 0.0) / scale
        residual = image - rayleigh * unit
        change = residual / (jnp.abs(diagonal - rayleigh) + 1.0)
        rounded = change.astype(BF16)
        for chip in range(NCHIP):
            spread_ref[chip, block * ROWS : (block + 1) * ROWS] = rounded
        if block < 2:
            image_ref[block] = image
            change_ref[block] = change
            again = rounded.astype(F32)
            amounts[0] = amounts[0] + diagonal * again * again
            amounts[1] = amounts[1] + unit * change
            amounts[2] = amounts[2] + change * change
            amounts[3] = amounts[3] + change * image
    scalar_ref[...] = lanes([total(amount) for amount in amounts], WIDTH)
    known_ref[...] = lanes([rayleigh, scale], 128)


def ritz_kernel(
    place_ref, size_ref, gathered_ref, known_ref, first_ref, second_ref, arrived_ref,
    diagonal_ref, rows_ref, image_ref, change_ref, vector_ref, residual_ref, energies_ref,
):
    change_energy, correlation, square, change_image = scalars_of(gathered_ref, 4)
    rayleigh = known_ref[:, 0:1]
    scale = known_ref[:, 1:2]
    spread = square - correlation * correlation
    deviation = jnp.sqrt(spread)
    cross_term = (change_image - correlation * rayleigh) / deviation
    second_energy = (
        change_energy - 2.0 * correlation * change_image + correlation * correlation * rayleigh
    ) / spread
    half_gap = 0.5 * (rayleigh - second_energy)
    length = jnp.sqrt(half_gap * half_gap + cross_term * cross_term)
    lowest = 0.5 * (rayleigh + second_energy) - length
    apart = length > 0.0
    divisor = jnp.where(apart, length, 1.0)
    double_cosine = jnp.where(apart, half_gap / divisor, 1.0)
    double_sine = jnp.where(apart, cross_term / divisor, 0.0)
    larger = jnp.sqrt(0.5 * (1.0 + jnp.abs(double_cosine)))
    smaller = 0.5 * double_sine / larger
    ahead = double_cosine >= 0.0
    sign = jnp.where(cross_term < 0.0, -1.0, 1.0)
    cosine_angle = jnp.where(ahead, larger, jnp.abs(smaller))
    sine_angle = jnp.where(ahead, smaller, sign * larger)
    first_row = group(place_ref[1], place_ref[0])
    sums = [first_ref[...] + arrived_ref[...], second_ref[...]]
    for block in range(2):
        mask = inside(size_of(place_ref, size_ref, block), first_row, (ROWS, WIDTH))
        unit = rows_ref[block] / scale
        image = image_ref[block]
        change = change_ref[block]
        rounded = change.astype(BF16).astype(F32)
        change_picture = jnp.where(mask, sums[block] + diagonal_ref[block] * rounded, 0.0)
        unit_second = (change - correlation * unit) / deviation
        second_image = (change_picture - correlation * image) / deviation
        ritz_unit = sine_angle * unit - cosine_angle * unit_second
        vector_ref[block] = (scale * ritz_unit).astype(BF16)
        residual_ref[block] = (
            scale * (sine_angle * image - cosine_angle * second_image - lowest * ritz_unit)
        ).astype(BF16)
    energies_ref[...] = lanes([rayleigh, lowest], 128)


def shaped(shape, dtype):
    return jax.ShapeDtypeStruct(shape, dtype)


def line(distance):
    devices = range(lax.axis_size(SEC))
    return [(i, i + distance) for i in devices if i + distance in devices]


def body(start, left, right, left_energy, right_energy, sector_size, sector_spin):
    core = lax.axis_index("c")
    chip = lax.axis_index(CHIPS)
    place = jnp.stack([core, chip, 2 * lax.axis_index(SEC)]).astype(jnp.int32)
    swap = [(0, 1), (1, 0)]
    halo = lax.ppermute(start[0], SEC, line(-1))
    levels = jnp.concatenate([left_energy[:1], right_energy[:1]]).reshape(8, 128)
    levels = lax.ppermute(levels, SEC, line(-1)).reshape(2, WIDTH)
    swapped = lax.ppermute(right, "c", swap)
    operators = shaped((4, HALF, WIDTH), BF16)
    keep, send = call(
        sort_kernel, (operators, operators), [SM, VM], [pltpu.VMEM((WIDTH, WIDTH), BF16)]
    )(place, left)
    other = lax.ppermute(send, "c", swap)
    left_levels = jnp.concatenate([left_energy, levels[:1]])
    right_levels = jnp.concatenate([right_energy, levels[1:]])
    own_levels = lax.dynamic_slice_in_dim(left_levels, (2 * chip + core) * ROWS, ROWS, 1)
    diagonal = own_levels[:, :, None] + right_levels[:, None, :]

    field = pltpu.VMEM((BLOCKS, WIDTH, WIDTH), BF16)
    parts_shape = shaped((NCHIP, PART, WIDTH), BF16)
    rows_shape = shaped((BLOCKS, ROWS, WIDTH), F32)
    own_shape = shaped((2, ROWS, WIDTH), F32)
    row_shape = shaped((ROWS, WIDTH), F32)
    many = lax.axis_size(("c",) + SEC)
    work = 32 * HALF * WIDTH * WIDTH

    def summed(parts):
        received = lax.all_to_all(parts, CHIPS, 0, 0)
        return call(
            sum_kernel, (row_shape, row_shape, row_shape, shaped((many, 8, 128), F32)), [VM]
        )(received)

    parts, rows = call(
        first_kernel, (parts_shape, rows_shape), [SM] * 3 + [VM] * 7, [field], work, 6 << 20
    )(place, sector_size, sector_spin, start, halo, diagonal, keep, other, right, swapped)
    first, second, leaving, scalars = summed(parts)
    gathered = lax.all_to_all(scalars, ("c",) + SEC, 0, 0)
    arrived = lax.ppermute(leaving, SEC, line(1))
    ahead = lax.ppermute(first, SEC, line(-1))
    spread, image, change, amounts, known = call(
        correction_kernel,
        (
            shaped((NCHIP, BLOCKS * ROWS, WIDTH), BF16), own_shape, own_shape,
            shaped((1, WIDTH), F32), shaped((1, 128), F32),
        ),
        [SM] * 2 + [VM] * 8,
    )(place, sector_size, gathered, first, second, leaving, arrived, ahead, diagonal, rows)
    near = lax.all_to_all(spread, CHIPS, 0, 0)
    far = lax.ppermute(near, "c", swap)
    parts = call(second_kernel, parts_shape, [SM] * 2 + [VM] * 7, [field], work, 6 << 20)(
        place, sector_spin, near, far, amounts, keep, other, right, swapped
    )
    first, second, leaving, scalars = summed(parts)
    gathered = lax.all_to_all(scalars, ("c",) + SEC, 0, 0)
    arrived = lax.ppermute(leaving, SEC, line(1))
    result = shaped((2, ROWS, WIDTH), BF16)
    vector, residual, energies = call(
        ritz_kernel, (result, result, shaped((1, 128), F32)), [SM] * 2 + [VM] * 9
    )(
        place, sector_size, gathered, known, first, second, arrived,
        diagonal, rows, image, change,
    )
    return vector, residual, energies[0, :2]


def solution(mesh):
    fine = Mesh(mesh.devices.reshape(2, 4, 2, 2, 16), ("yh", "x", "c", "yl", "z"))
    return jax.shard_map(
        body,
        mesh=fine,
        in_specs=(
            P(SEC, None, None),
            P(OP, SEC, None, None),
            P(OP, SEC, None, None),
            P(SEC, None),
            P(SEC, None),
            P(),
            P(),
        ),
        out_specs=(P(SEC, OP, None), P(SEC, OP, None), P()),
        check_vma=False,
    )
```

```python
import functools

import jax
import jax.numpy as jnp
from jax import lax
from jax.experimental import pallas as pl
from jax.experimental.pallas import tpu as pltpu
from jax.sharding import Mesh, PartitionSpec as P

F32 = jnp.float32
BF16 = jnp.bfloat16
OP = ("yh", "x", "c")
CHIPS = ("yh", "x")
SEC = ("yl", "z")
WIDTH = 512
ROWS = 32
HALF = 256
NCHIP = 8
BLOCKS = 3
PART = BLOCKS * ROWS + 16
VMEM_LIMIT = 48 * 1024 * 1024


def call(kernel, out_shape, in_specs, scratch=(), flops=0, nbytes=1 << 20):
    return pl.pallas_call(
        kernel,
        out_shape=out_shape,
        in_specs=in_specs,
        out_specs=jax.tree.map(lambda _: pl.BlockSpec(memory_space=pltpu.VMEM), out_shape),
        scratch_shapes=list(scratch),
        compiler_params=pltpu.CompilerParams(vmem_limit_bytes=VMEM_LIMIT),
        cost_estimate=pl.CostEstimate(flops=flops, bytes_accessed=nbytes, transcendentals=0),
    )


VM = pl.BlockSpec(memory_space=pltpu.VMEM)
SM = pl.BlockSpec(memory_space=pltpu.SMEM)


def product(first, second, second_axis=0):
    return lax.dot_general(
        first, second, (((1,), (second_axis,)), ((), ())), preferred_element_type=F32
    )


def group(chip, core):
    return pl.multiple_of((2 * chip + core) * ROWS, ROWS)


def total(array):
    return jnp.sum(jnp.sum(array, axis=0, keepdims=True), axis=1, keepdims=True)


def lanes(values, width):
    place = lax.broadcasted_iota(jnp.int32, (1, width), 1)
    row = jnp.zeros((1, width), F32)
    for index, value in enumerate(values):
        row = jnp.where(place == index, value, row)
    return row


def sort_kernel(place_ref, left_ref, keep_ref, send_ref, turned):
    core = place_ref[0]
    for sector in range(2):
        turned[...] = left_ref[0, sector].T
        for chip in range(NCHIP):
            here = pl.ds(chip * ROWS, ROWS)
            keep_ref[sector, here] = left_ref[0, sector, pl.ds(group(chip, core), ROWS)]
            send_ref[sector, here] = left_ref[0, sector, pl.ds(group(chip, 1 - core), ROWS)]
            keep_ref[2 + sector, here] = turned[pl.ds(group(chip, core), ROWS)]
            send_ref[2 + sector, here] = turned[pl.ds(group(chip, 1 - core), ROWS)]


def image_blocks(place_ref, spin_ref, keep_ref, other_ref, right_ref, swapped_ref, field):
    first = place_ref[2]
    blocks = [None, None, None]
    for sector in range(2):
        here = first + sector
        following = jnp.minimum(here + 1, spin_ref.shape[0] - 1)
        above = jnp.full((1, WIDTH), spin_ref[following], jnp.int32).astype(F32) + 1.0
        below = jnp.full((1, WIDTH), spin_ref[here], jnp.int32).astype(F32) + 1.0
        linked = jnp.full((1, WIDTH), here, jnp.int32) + 1 < spin_ref.shape[0]
        coupling = jnp.where(linked, jnp.sqrt(above / below), 0.0)
        lowered = raised = None
        for left, right in ((keep_ref, right_ref.at[0]), (other_ref, swapped_ref.at[0])):
            left_image = product(left[2 + sector], field[sector + 1]).astype(BF16)
            down = product(left_image, right[sector])
            left_product = product(left[sector], field[sector]).astype(BF16)
            up = product(left_product, right[sector], 1)
            lowered = down if lowered is None else lowered + down
            raised = up if raised is None else raised + up
        lowered = coupling * lowered
        blocks[sector] = lowered if blocks[sector] is None else blocks[sector] + lowered
        blocks[sector + 1] = coupling * raised
    return blocks


def put_parts(place_ref, blocks, field, scalars, parts_ref):
    core = place_ref[0]
    energy = jnp.zeros((ROWS, WIDTH), F32)
    for index, block in enumerate(blocks):
        rounded = block.astype(BF16)
        for chip in range(NCHIP):
            piece = rounded[chip * ROWS : (chip + 1) * ROWS]
            parts_ref[chip, index * ROWS : (index + 1) * ROWS] = piece
            own = field[index, pl.ds(group(chip, core), ROWS)]
            energy = energy + piece.astype(F32) * own.astype(F32)
    row = lanes([total(energy)], WIDTH) + scalars
    high = row.astype(BF16)
    rest = row - high.astype(F32)
    middle = rest.astype(BF16)
    low = (rest - middle.astype(F32)).astype(BF16)
    place = lax.broadcasted_iota(jnp.int32, (16, WIDTH), 0)
    coded = jnp.where(
        place == 0,
        high.astype(F32),
        jnp.where(place == 1, middle.astype(F32), jnp.where(place == 2, low.astype(F32), 0.0)),
    ).astype(BF16)
    for chip in range(NCHIP):
        parts_ref[chip, BLOCKS * ROWS :] = coded


def inside(size, first_row, shape):
    rows = lax.broadcasted_iota(jnp.int32, shape, 0) + first_row
    columns = lax.broadcasted_iota(jnp.int32, shape, 1)
    return (rows < size) & (columns < size)


def size_of(place_ref, size_ref, block):
    return size_ref[jnp.minimum(place_ref[2] + block, size_ref.shape[0] - 1)]


def mask_kernel(place_ref, size_ref, start_ref, halo_ref, field_ref):
    for block in range(BLOCKS):
        source = halo_ref[...] if block == 2 else start_ref[block]
        mask = inside(size_of(place_ref, size_ref, block), 0, (WIDTH, WIDTH))
        field_ref[block] = jnp.where(mask, source.astype(F32), 0.0).astype(BF16)


def first_kernel(
    place_ref, spin_ref, field, diagonal_ref,
    keep_ref, other_ref, right_ref, swapped_ref, parts_ref, rows_ref,
):
    norm = jnp.zeros((ROWS, WIDTH), F32)
    energy = jnp.zeros((ROWS, WIDTH), F32)
    for block in range(BLOCKS):
        own = field[block, pl.ds(group(place_ref[1], place_ref[0]), ROWS)].astype(F32)
        rows_ref[block] = own
        if block < 2:
            norm = norm + own * own
            energy = energy + diagonal_ref[block] * (own * own)
    blocks = image_blocks(place_ref, spin_ref, keep_ref, other_ref, right_ref, swapped_ref, field)
    put_parts(place_ref, blocks, field, lanes([total(energy), total(norm)], WIDTH), parts_ref)


def second_kernel(
    place_ref, spin_ref, near_ref, far_ref, scalar_ref,
    keep_ref, other_ref, right_ref, swapped_ref, parts_ref, field,
):
    core = place_ref[0]
    for chip in range(NCHIP):
        for block in range(BLOCKS):
            there = pl.ds(block * ROWS, ROWS)
            field[block, pl.ds(group(chip, core), ROWS)] = near_ref[chip, there]
            field[block, pl.ds(group(chip, 1 - core), ROWS)] = far_ref[chip, there]
    blocks = image_blocks(place_ref, spin_ref, keep_ref, other_ref, right_ref, swapped_ref, field)
    put_parts(place_ref, blocks, field, scalar_ref[...], parts_ref)


def sum_kernel(received_ref, first_ref, second_ref, leaving_ref, scalar_ref):
    for index, out_ref in enumerate((first_ref, second_ref, leaving_ref)):
        running = jnp.zeros((ROWS, WIDTH), F32)
        for chip in range(NCHIP):
            running = running + received_ref[chip, index * ROWS : (index + 1) * ROWS].astype(F32)
        out_ref[...] = running
    coded = jnp.zeros((16, WIDTH), F32)
    for chip in range(NCHIP):
        coded = coded + received_ref[chip, BLOCKS * ROWS :].astype(F32)
    row = jnp.sum(coded, axis=0, keepdims=True)[:, :128]
    scalar_ref[...] = jnp.broadcast_to(row[None], scalar_ref.shape)


def scalars_of(gathered_ref, count):
    row = jnp.sum(gathered_ref[...], axis=0)
    return [row[:, index : index + 1] for index in range(count)]


def correction_kernel(
    place_ref, size_ref, gathered_ref, first_ref, second_ref, leaving_ref, arrived_ref,
    ahead_ref, diagonal_ref, next_ref, rows_ref, spread_ref, image_ref, change_ref, scalar_ref, known_ref,
):
    energy, norm = scalars_of(gathered_ref, 2)
    rayleigh = energy / norm
    scale = jnp.sqrt(norm)
    first_row = group(place_ref[1], place_ref[0])
    sums = [first_ref[...] + arrived_ref[...], second_ref[...], leaving_ref[...] + ahead_ref[...]]
    amounts = [jnp.zeros((ROWS, WIDTH), F32) for _ in range(4)]
    for block in range(BLOCKS):
        mask = inside(size_of(place_ref, size_ref, block), first_row, (ROWS, WIDTH))
        values = rows_ref[block]
        diagonal = next_ref[...] if block == 2 else diagonal_ref[block]
        unit = values / scale
        image = jnp.where(mask, sums[block] + diagonal * values, 0.0) / scale
        residual = image - rayleigh * unit
        change = residual / (jnp.abs(diagonal - rayleigh) + 1.0)
        rounded = change.astype(BF16)
        for chip in range(NCHIP):
            spread_ref[chip, block * ROWS : (block + 1) * ROWS] = rounded
        if block < 2:
            image_ref[block] = image
            change_ref[block] = change
            again = rounded.astype(F32)
            amounts[0] = amounts[0] + diagonal * again * again
            amounts[1] = amounts[1] + unit * change
            amounts[2] = amounts[2] + change * change
            amounts[3] = amounts[3] + change * image
    scalar_ref[...] = lanes([total(amount) for amount in amounts], WIDTH)
    known_ref[...] = lanes([rayleigh, scale], 128)


def ritz_kernel(
    place_ref, size_ref, gathered_ref, known_ref, first_ref, second_ref, arrived_ref,
    diagonal_ref, rows_ref, image_ref, change_ref, vector_ref, residual_ref, energies_ref,
):
    change_energy, correlation, square, change_image = scalars_of(gathered_ref, 4)
    rayleigh = known_ref[:, 0:1]
    scale = known_ref[:, 1:2]
    spread = square - correlation * correlation
    deviation = jnp.sqrt(spread)
    cross_term = (change_image - correlation * rayleigh) / deviation
    second_energy = (
        change_energy - 2.0 * correlation * change_image + correlation * correlation * rayleigh
    ) / spread
    half_gap = 0.5 * (rayleigh - second_energy)
    length = jnp.sqrt(half_gap * half_gap + cross_term * cross_term)
    lowest = 0.5 * (rayleigh + second_energy) - length
    apart = length > 0.0
    divisor = jnp.where(apart, length, 1.0)
    double_cosine = jnp.where(apart, half_gap / divisor, 1.0)
    double_sine = jnp.where(apart, cross_term / divisor, 0.0)
    larger = jnp.sqrt(0.5 * (1.0 + jnp.abs(double_cosine)))
    smaller = 0.5 * double_sine / larger
    ahead = double_cosine >= 0.0
    sign = jnp.where(cross_term < 0.0, -1.0, 1.0)
    cosine_angle = jnp.where(ahead, larger, jnp.abs(smaller))
    sine_angle = jnp.where(ahead, smaller, sign * larger)
    first_row = group(place_ref[1], place_ref[0])
    sums = [first_ref[...] + arrived_ref[...], second_ref[...]]
    for block in range(2):
        mask = inside(size_of(place_ref, size_ref, block), first_row, (ROWS, WIDTH))
        unit = rows_ref[block] / scale
        image = image_ref[block]
        change = change_ref[block]
        rounded = change.astype(BF16).astype(F32)
        change_picture = jnp.where(mask, sums[block] + diagonal_ref[block] * rounded, 0.0)
        unit_second = (change - correlation * unit) / deviation
        second_image = (change_picture - correlation * image) / deviation
        ritz_unit = sine_angle * unit - cosine_angle * unit_second
        vector_ref[block] = (scale * ritz_unit).astype(BF16)
        residual_ref[block] = (
            scale * (sine_angle * image - cosine_angle * second_image - lowest * ritz_unit)
        ).astype(BF16)
    energies_ref[...] = lanes([rayleigh, lowest], 128)


def shaped(shape, dtype):
    return jax.ShapeDtypeStruct(shape, dtype)


def line(distance):
    devices = range(lax.axis_size(SEC))
    return [(i, i + distance) for i in devices if i + distance in devices]


def body(start, left, right, left_energy, right_energy, sector_size, sector_spin):
    core = lax.axis_index("c")
    chip = lax.axis_index(CHIPS)
    place = jnp.stack([core, chip, 2 * lax.axis_index(SEC)]).astype(jnp.int32)
    swap = [(0, 1), (1, 0)]
    halo = lax.ppermute(start[0], SEC, line(-1))
    levels = jnp.concatenate([left_energy[:1], right_energy[:1]]).reshape(8, 128)
    levels = lax.ppermute(levels, SEC, line(-1)).reshape(2, WIDTH)
    first_row = (2 * chip + core) * ROWS

    def diagonal_rows(left_levels, right_levels):
        own_levels = lax.dynamic_slice_in_dim(left_levels, first_row, ROWS, 1)
        return own_levels[:, :, None] + right_levels[:, None, :]

    swapped = lax.ppermute(right, "c", swap)
    operators = shaped((4, HALF, WIDTH), BF16)
    keep, send = call(
        sort_kernel, (operators, operators), [SM, VM], [pltpu.VMEM((WIDTH, WIDTH), BF16)]
    )(place, left)
    other = lax.ppermute(send, "c", swap)
    diagonal = diagonal_rows(left_energy, right_energy)
    next_diagonal = diagonal_rows(levels[:1], levels[1:])[0]

    field = pltpu.VMEM((BLOCKS, WIDTH, WIDTH), BF16)
    parts_shape = shaped((NCHIP, PART, WIDTH), BF16)
    rows_shape = shaped((BLOCKS, ROWS, WIDTH), F32)
    own_shape = shaped((2, ROWS, WIDTH), F32)
    row_shape = shaped((ROWS, WIDTH), F32)
    many = lax.axis_size(("c",) + SEC)
    work = 32 * HALF * WIDTH * WIDTH

    def summed(parts):
        received = lax.all_to_all(parts, CHIPS, 0, 0)
        return call(
            sum_kernel, (row_shape, row_shape, row_shape, shaped((many, 1, 128), F32)), [VM]
        )(received)

    masked = call(
        mask_kernel, shaped((BLOCKS, WIDTH, WIDTH), BF16), [SM] * 2 + [VM] * 2, (), 4 * work, 3 << 20
    )(place, sector_size, start, halo)
    parts, rows = call(
        first_kernel, (parts_shape, rows_shape), [SM] * 2 + [VM] * 6, (), work, 6 << 20
    )(place, sector_spin, masked, diagonal, keep, other, right, swapped)
    first, second, leaving, scalars = summed(parts)
    gathered = lax.all_to_all(scalars, ("c",) + SEC, 0, 0)
    arrived = lax.ppermute(leaving, SEC, line(1))
    ahead = lax.ppermute(first, SEC, line(-1))
    spread, image, change, amounts, known = call(
        correction_kernel,
        (
            shaped((NCHIP, BLOCKS * ROWS, WIDTH), BF16), own_shape, own_shape,
            shaped((1, WIDTH), F32), shaped((1, 128), F32),
        ),
        [SM] * 2 + [VM] * 9,
    )(
        place, sector_size, gathered, first, second, leaving, arrived, ahead,
        diagonal, next_diagonal, rows,
    )
    near = lax.all_to_all(spread, CHIPS, 0, 0)
    far = lax.ppermute(near, "c", swap)
    parts = call(second_kernel, parts_shape, [SM] * 2 + [VM] * 7, [field], work, 6 << 20)(
        place, sector_spin, near, far, amounts, keep, other, right, swapped
    )
    first, second, leaving, scalars = summed(parts)
    gathered = lax.all_to_all(scalars, ("c",) + SEC, 0, 0)
    arrived = lax.ppermute(leaving, SEC, line(1))
    result = shaped((2, ROWS, WIDTH), BF16)
    vector, residual, energies = call(
        ritz_kernel, (result, result, shaped((1, 128), F32)), [SM] * 2 + [VM] * 9
    )(
        place, sector_size, gathered, known, first, second, arrived,
        diagonal, rows, image, change,
    )
    return vector, residual, energies[0, :2]


def solution(mesh):
    fine = Mesh(mesh.devices.reshape(2, 4, 2, 2, 16), ("yh", "x", "c", "yl", "z"))
    return jax.shard_map(
        body,
        mesh=fine,
        in_specs=(
            P(SEC, None, None),
            P(OP, SEC, None, None),
            P(OP, SEC, None, None),
            P(SEC, None),
            P(SEC, None),
            P(),
            P(),
        ),
        out_specs=(P(SEC, OP, None), P(SEC, OP, None), P()),
        check_vma=False,
    )
```

```python
import jax
import jax.numpy as jnp
from jax import lax
from jax.experimental import pallas as pl
from jax.experimental.pallas import tpu as pltpu
from jax.sharding import Mesh, PartitionSpec as P

F32 = jnp.float32
BF16 = jnp.bfloat16
OP = ("yh", "x", "c")
SEC = ("yl", "z")
WIDTH = 512
ROWS = 32
NOP = 16
BLOCKS = 3
PART = 2 * ROWS + 8
VMEM_LIMIT = 24 * 1024 * 1024

VM = pl.BlockSpec(memory_space=pltpu.VMEM)
SM = pl.BlockSpec(memory_space=pltpu.SMEM)
HBM = pl.BlockSpec(memory_space=pltpu.HBM)


def call(kernel, out_shape, in_specs, scratch=(), flops=0, nbytes=1 << 20, out_spec=VM):
    return pl.pallas_call(
        kernel,
        out_shape=out_shape,
        in_specs=in_specs,
        out_specs=jax.tree.map(lambda _: out_spec, out_shape),
        scratch_shapes=list(scratch),
        compiler_params=pltpu.CompilerParams(vmem_limit_bytes=VMEM_LIMIT),
        cost_estimate=pl.CostEstimate(flops=flops, bytes_accessed=nbytes, transcendentals=0),
    )


def shaped(shape, dtype):
    return jax.ShapeDtypeStruct(shape, dtype)


def product(first, second, second_axis=0):
    return lax.dot_general(
        first, second, (((1,), (second_axis,)), ((), ())), preferred_element_type=F32
    )


def total(array):
    return jnp.sum(jnp.sum(array, axis=0, keepdims=True), axis=1, keepdims=True)


def lanes(values, width):
    place = lax.broadcasted_iota(jnp.int32, (1, width), 1)
    row = jnp.zeros((1, width), F32)
    for index, value in enumerate(values):
        row = jnp.where(place == index, value, row)
    return row


def own_rows(place_ref):
    return pl.multiple_of(place_ref[1] * ROWS, ROWS)


def inside(size, first_row, shape):
    rows = lax.broadcasted_iota(jnp.int32, shape, 0) + first_row
    columns = lax.broadcasted_iota(jnp.int32, shape, 1)
    return (rows < size) & (columns < size)


def size_of(place_ref, size_ref, block):
    return size_ref[jnp.minimum(place_ref[2] + block, size_ref.shape[0] - 1)]


def send_kernel(place_ref, start_ref, left_ref, right_ref, halo_ref, send_ref, semaphores):
    there = 1 - place_ref[0]
    copies = [
        pltpu.make_async_copy(start_ref.at[0], halo_ref, semaphores.at[0]),
        pltpu.make_async_copy(left_ref.at[0, there], send_ref.at[0], semaphores.at[1]),
        pltpu.make_async_copy(right_ref.at[0, there], send_ref.at[1], semaphores.at[2]),
    ]
    for copy in copies:
        copy.start()
    for copy in copies:
        copy.wait()


def mask_kernel(place_ref, size_ref, start_ref, halo_ref, field_ref, rows_ref):
    core = place_ref[0]

    def masked(source, block, first_row=0):
        mask = inside(size_of(place_ref, size_ref, block), first_row, source.shape)
        return jnp.where(mask, source.astype(F32), 0.0)

    field_ref[0] = masked(start_ref[core], core).astype(BF16)

    @pl.when(core == 0)
    def _():
        field_ref[1] = masked(start_ref[1], 1).astype(BF16)

    @pl.when(core == 1)
    def _():
        field_ref[1] = masked(halo_ref[...], 2).astype(BF16)

    first_row = own_rows(place_ref)
    for block in range(2):
        rows_ref[block] = masked(start_ref[block, pl.ds(first_row, ROWS)], block, first_row)


def images(place_ref, spin_ref, left_ref, right_ref, other_ref, field, after):
    core = place_ref[0]
    here = place_ref[2] + core
    following = jnp.minimum(here + 1, spin_ref.shape[0] - 1)
    above = jnp.full((1, WIDTH), spin_ref[following], jnp.int32).astype(F32) + 1.0
    below = jnp.full((1, WIDTH), spin_ref[here], jnp.int32).astype(F32) + 1.0
    linked = jnp.full((1, WIDTH), here, jnp.int32) + 1 < spin_ref.shape[0]
    coupling = jnp.where(linked, jnp.sqrt(above / below), 0.0)
    lowered = raised = None
    for left, right in (
        (left_ref[0, core], right_ref[0, core]),
        (other_ref[0], other_ref[1]),
    ):
        up = product(left, product(field, right, 1).astype(BF16))
        down = product(product(left.T, after).astype(BF16), right)
        raised = up if raised is None else raised + up
        lowered = down if lowered is None else lowered + down
    return coupling * lowered, coupling * raised


def put_parts(lowered, raised, after, scalars, parts_ref):
    energy = 2.0 * total(raised * after.astype(F32))
    row = lanes([energy], WIDTH) + scalars
    high = row.astype(BF16).astype(F32)
    middle = (row - high).astype(BF16).astype(F32)
    low = (row - high) - middle
    place = lax.broadcasted_iota(jnp.int32, (8, WIDTH), 0)
    coded = jnp.where(
        place == 0, high, jnp.where(place == 1, middle, jnp.where(place == 2, low, 0.0))
    ).astype(BF16)
    for device in range(NOP):
        here = slice(device * ROWS, (device + 1) * ROWS)
        parts_ref[device, :ROWS] = lowered[here].astype(BF16)
        parts_ref[device, ROWS : 2 * ROWS] = raised[here].astype(BF16)
        parts_ref[device, 2 * ROWS :] = coded


def first_kernel(
    place_ref, spin_ref, field_ref, rows_ref, diagonal_ref, left_ref, right_ref, other_ref, parts_ref
):
    norm = jnp.zeros((ROWS, WIDTH), F32)
    energy = jnp.zeros((ROWS, WIDTH), F32)
    for block in range(2):
        square = rows_ref[block] * rows_ref[block]
        norm = norm + square
        energy = energy + diagonal_ref[block] * square
    after = field_ref[1]
    lowered, raised = images(
        place_ref, spin_ref, left_ref, right_ref, other_ref, field_ref[0], after
    )
    put_parts(lowered, raised, after, lanes([total(energy), total(norm)], WIDTH), parts_ref)


def second_kernel(
    place_ref, spin_ref, gathered_ref, scalar_ref, left_ref, right_ref, other_ref, parts_ref
):
    field = gathered_ref[:, :ROWS].reshape(WIDTH, WIDTH)
    after = gathered_ref[:, ROWS:].reshape(WIDTH, WIDTH)
    lowered, raised = images(place_ref, spin_ref, left_ref, right_ref, other_ref, field, after)
    put_parts(lowered, raised, after, scalar_ref[...], parts_ref)


def scalar_kernel(received_ref, scalar_ref):
    coded = jnp.zeros((8, 128), F32)
    for device in range(NOP):
        coded = coded + received_ref[device, 2 * ROWS :, :128].astype(F32)
    row = jnp.sum(coded, axis=0, keepdims=True)
    scalar_ref[...] = jnp.broadcast_to(row[None], scalar_ref.shape)


def sum_kernel(received_ref, first_ref, second_ref, leaving_ref):
    sums = [jnp.zeros((ROWS, WIDTH), F32) for _ in range(BLOCKS)]
    for device in range(NOP):
        block = device % 2
        sums[block] = sums[block] + received_ref[device, :ROWS].astype(F32)
        sums[block + 1] = sums[block + 1] + received_ref[device, ROWS : 2 * ROWS].astype(F32)
    first_ref[...], second_ref[...], leaving_ref[...] = sums


def scalars_of(gathered_ref, count):
    row = jnp.sum(gathered_ref[...], axis=0)
    return [row[:, index : index + 1] for index in range(count)]


def correction_kernel(
    place_ref, size_ref, gathered_ref, first_ref, second_ref, leaving_ref, arrived_ref,
    ahead_ref, diagonal_ref, next_diagonal_ref, rows_ref, next_rows_ref,
    spread_ref, image_ref, change_ref, scalar_ref, known_ref,
):
    energy, norm = scalars_of(gathered_ref, 2)
    rayleigh = energy / norm
    scale = jnp.sqrt(norm)
    first_row = own_rows(place_ref)
    sums = [first_ref[...] + arrived_ref[...], second_ref[...], leaving_ref[...] + ahead_ref[...]]
    amounts = [jnp.zeros((ROWS, WIDTH), F32) for _ in range(4)]
    for block in range(BLOCKS):
        mask = inside(size_of(place_ref, size_ref, block), first_row, (ROWS, WIDTH))
        values = next_rows_ref[:ROWS] if block == 2 else rows_ref[block]
        diagonal = next_diagonal_ref[...] if block == 2 else diagonal_ref[block]
        unit = jnp.where(mask, values, 0.0) / scale
        image = jnp.where(mask, sums[block] + diagonal * values, 0.0) / scale
        residual = image - rayleigh * unit
        change = residual / (jnp.abs(diagonal - rayleigh) + 1.0)
        rounded = change.astype(BF16)
        for device in range(NOP):
            part = block - device % 2
            if part in (0, 1):
                spread_ref[device, part * ROWS : (part + 1) * ROWS] = rounded
        if block < 2:
            image_ref[block] = image
            change_ref[block] = change
            again = rounded.astype(F32)
            amounts[0] = amounts[0] + diagonal * again * again
            amounts[1] = amounts[1] + unit * change
            amounts[2] = amounts[2] + change * change
            amounts[3] = amounts[3] + change * image
    scalar_ref[...] = lanes([total(amount) for amount in amounts], WIDTH)
    known_ref[...] = lanes([rayleigh, scale], 128)


def ritz_kernel(
    place_ref, size_ref, gathered_ref, known_ref, first_ref, second_ref, arrived_ref,
    diagonal_ref, rows_ref, image_ref, change_ref, vector_ref, residual_ref, energies_ref,
):
    change_energy, correlation, square, change_image = scalars_of(gathered_ref, 4)
    rayleigh = known_ref[:, 0:1]
    scale = known_ref[:, 1:2]
    spread = square - correlation * correlation
    deviation = jnp.sqrt(spread)
    cross_term = (change_image - correlation * rayleigh) / deviation
    second_energy = (
        change_energy - 2.0 * correlation * change_image + correlation * correlation * rayleigh
    ) / spread
    half_gap = 0.5 * (rayleigh - second_energy)
    length = jnp.sqrt(half_gap * half_gap + cross_term * cross_term)
    lowest = 0.5 * (rayleigh + second_energy) - length
    apart = length > 0.0
    divisor = jnp.where(apart, length, 1.0)
    double_cosine = jnp.where(apart, half_gap / divisor, 1.0)
    double_sine = jnp.where(apart, cross_term / divisor, 0.0)
    larger = jnp.sqrt(0.5 * (1.0 + jnp.abs(double_cosine)))
    smaller = 0.5 * double_sine / larger
    ahead = double_cosine >= 0.0
    sign = jnp.where(cross_term < 0.0, -1.0, 1.0)
    cosine_angle = jnp.where(ahead, larger, jnp.abs(smaller))
    sine_angle = jnp.where(ahead, smaller, sign * larger)
    first_row = own_rows(place_ref)
    sums = [first_ref[...] + arrived_ref[...], second_ref[...]]
    for block in range(2):
        mask = inside(size_of(place_ref, size_ref, block), first_row, (ROWS, WIDTH))
        unit = rows_ref[block] / scale
        image = image_ref[block]
        change = change_ref[block]
        rounded = change.astype(BF16).astype(F32)
        change_picture = jnp.where(mask, sums[block] + diagonal_ref[block] * rounded, 0.0)
        unit_second = (change - correlation * unit) / deviation
        second_image = (change_picture - correlation * image) / deviation
        ritz_unit = sine_angle * unit - cosine_angle * unit_second
        vector_ref[block] = (scale * ritz_unit).astype(BF16)
        residual_ref[block] = (
            scale * (sine_angle * image - cosine_angle * second_image - lowest * ritz_unit)
        ).astype(BF16)
    energies_ref[...] = lanes([rayleigh, lowest], 2)


def line(distance):
    devices = range(lax.axis_size(SEC))
    return [(i, i + distance) for i in devices if i + distance in devices]


def body(start, left, right, left_energy, right_energy, sector_size, sector_spin):
    core = lax.axis_index("c")
    position = lax.axis_index(OP)
    sectors = lax.axis_size(SEC)
    place = jnp.stack([core, position, 2 * lax.axis_index(SEC)]).astype(jnp.int32)
    block_shape = shaped((WIDTH, WIDTH), BF16)
    own_shape = shaped((2, ROWS, WIDTH), F32)
    row_shape = shaped((ROWS, WIDTH), F32)
    parts_shape = shaped((NOP, PART, WIDTH), BF16)
    work = 16 * WIDTH * WIDTH * WIDTH

    halo_source, send = call(
        send_kernel,
        (block_shape, shaped((2, WIDTH, WIDTH), BF16)),
        [SM, HBM, HBM, HBM],
        [pltpu.SemaphoreType.DMA((3,))],
        out_spec=HBM,
    )(place, start, left, right)
    to_second_core = [(sectors + i + 1, sectors + i) for i in range(sectors - 1)]
    halo = lax.ppermute(halo_source, ("c",) + SEC, to_second_core)
    other = lax.ppermute(send, "c", [(0, 1), (1, 0)])

    first_row = position * ROWS

    def diagonal_rows(left_levels, right_levels):
        own_levels = lax.dynamic_slice_in_dim(left_levels, first_row, ROWS, 1)
        return own_levels[:, :, None] + right_levels[:, None, :]

    diagonal = diagonal_rows(left_energy, right_energy)
    before = jnp.concatenate(
        [
            lax.dynamic_slice_in_dim(start[0], first_row, ROWS, 0).astype(F32),
            left_energy[:1],
            right_energy[:1],
            jnp.zeros((6, WIDTH), F32),
        ]
    )
    beyond = lax.ppermute(before, SEC, line(-1))
    next_diagonal = diagonal_rows(beyond[ROWS : ROWS + 1], beyond[ROWS + 1 : ROWS + 2])[0]

    def summed(parts):
        received = lax.all_to_all(parts, OP, 0, 0)
        scalars = call(scalar_kernel, shaped((sectors, 1, 128), F32), [VM])(received)
        gathered = lax.all_to_all(scalars, SEC, 0, 0)
        sums = call(sum_kernel, (row_shape, row_shape, row_shape), [VM])(received)
        return (*sums, gathered)

    field, rows = call(
        mask_kernel,
        (shaped((2, WIDTH, WIDTH), BF16), own_shape),
        [SM] * 2 + [VM] * 2,
        flops=4 * work,
        nbytes=3 << 20,
    )(place, sector_size, start, halo)
    parts = call(first_kernel, parts_shape, [SM] * 2 + [VM] * 6, flops=work, nbytes=4 << 20)(
        place, sector_spin, field, rows, diagonal, left, right, other
    )
    first, second, leaving, gathered = summed(parts)
    arrived = lax.ppermute(leaving, SEC, line(1))
    ahead = lax.ppermute(first, SEC, line(-1))
    spread, image, change, amounts, known = call(
        correction_kernel,
        (
            shaped((NOP, 2 * ROWS, WIDTH), BF16), own_shape, own_shape,
            shaped((1, WIDTH), F32), shaped((1, 128), F32),
        ),
        [SM] * 2 + [VM] * 10,
    )(
        place, sector_size, gathered, first, second, leaving, arrived, ahead,
        diagonal, next_diagonal, rows, beyond,
    )
    fields = lax.all_to_all(spread, OP, 0, 0)
    parts = call(second_kernel, parts_shape, [SM] * 2 + [VM] * 5, flops=work, nbytes=4 << 20)(
        place, sector_spin, fields, amounts, left, right, other
    )
    first, second, leaving, gathered = summed(parts)
    arrived = lax.ppermute(leaving, SEC, line(1))
    result = shaped((2, ROWS, WIDTH), BF16)
    vector, residual, energies = call(
        ritz_kernel, (result, result, shaped((1, 2), F32)), [SM] * 2 + [VM] * 9
    )(
        place, sector_size, gathered, known, first, second, arrived,
        diagonal, rows, image, change,
    )
    return vector, residual, energies.reshape(2)


def solution(mesh):
    fine = Mesh(mesh.devices.reshape(2, 4, 2, 2, 16), ("yh", "x", "c", "yl", "z"))
    return jax.shard_map(
        body,
        mesh=fine,
        in_specs=(
            P(SEC, None, None),
            P(OP, SEC, None, None),
            P(OP, SEC, None, None),
            P(SEC, None),
            P(SEC, None),
            P(),
            P(),
        ),
        out_specs=(P(SEC, OP, None), P(SEC, OP, None), P()),
        check_vma=False,
    )
```

```python
import jax
import jax.numpy as jnp
from jax import lax
from jax.experimental import pallas as pl
from jax.experimental.pallas import tpu as pltpu
from jax.sharding import Mesh, PartitionSpec as P

F32 = jnp.float32
BF16 = jnp.bfloat16
OP = ("yh", "x", "c")
SEC = ("yl", "z")
WIDTH = 512
ROWS = 32
NOP = 16
BLOCKS = 3
LANES = 128
TILES = WIDTH // LANES
PART = 2 * ROWS * TILES + 16
VMEM_LIMIT = 24 * 1024 * 1024
WHOLE_VMEM = 62 * 1024 * 1024

VM = pl.BlockSpec(memory_space=pltpu.VMEM)
SM = pl.BlockSpec(memory_space=pltpu.SMEM)
HBM = pl.BlockSpec(memory_space=pltpu.HBM)


def call(
    kernel, out_shape, in_specs, scratch=(), flops=0, nbytes=1 << 20, vmem=VMEM_LIMIT
):
    return pl.pallas_call(
        kernel,
        out_shape=out_shape,
        in_specs=in_specs,
        out_specs=jax.tree.map(lambda _: VM, out_shape),
        scratch_shapes=list(scratch),
        compiler_params=pltpu.CompilerParams(vmem_limit_bytes=vmem),
        cost_estimate=pl.CostEstimate(flops=flops, bytes_accessed=nbytes, transcendentals=0),
    )


def shaped(shape, dtype):
    return jax.ShapeDtypeStruct(shape, dtype)


def product(first, second, second_axis=0):
    return lax.dot_general(
        first, second, (((1,), (second_axis,)), ((), ())), preferred_element_type=F32
    )


def total(array):
    return jnp.sum(jnp.sum(array, axis=0, keepdims=True), axis=1, keepdims=True)


def lanes(values, width):
    place = lax.broadcasted_iota(jnp.int32, (1, width), 1)
    row = jnp.zeros((1, width), F32)
    for index, value in enumerate(values):
        row = jnp.where(place == index, value, row)
    return row


def own_rows(place_ref):
    return pl.multiple_of(place_ref[1] * ROWS, ROWS)


def inside(size, first_row, shape):
    rows = lax.broadcasted_iota(jnp.int32, shape, 0) + first_row
    columns = lax.broadcasted_iota(jnp.int32, shape, 1)
    return (rows < size) & (columns < size)


def size_of(place_ref, size_ref, block):
    return size_ref[jnp.minimum(place_ref[2] + block, size_ref.shape[0] - 1)]


def diagonal_of(left_row, right_row, first_row):
    rows = lax.broadcasted_iota(jnp.int32, (ROWS, WIDTH), 0) + first_row
    columns = lax.broadcasted_iota(jnp.int32, (ROWS, WIDTH), 1)
    chosen = jnp.where(rows == columns, left_row, 0.0)
    return jnp.sum(chosen, axis=1, keepdims=True) + right_row


def open_kernel(start_ref, left_ref, right_ref, halo_ref, send_ref, semaphores):
    there = 1 - lax.axis_index("c")
    copies = [
        pltpu.make_async_copy(start_ref.at[0], halo_ref, semaphores.at[0]),
        pltpu.make_async_copy(left_ref.at[0, there], send_ref.at[0], semaphores.at[1]),
        pltpu.make_async_copy(right_ref.at[0, there], send_ref.at[1], semaphores.at[2]),
    ]
    for copy in copies:
        copy.start()
    for copy in copies:
        copy.wait()


def rows_kernel(
    place_ref, size_ref, start_ref, left_levels_ref, right_levels_ref,
    rows_ref, diagonal_ref, scalar_ref, before_ref,
):
    first_row = own_rows(place_ref)
    norm = jnp.zeros((ROWS, WIDTH), F32)
    energy = jnp.zeros((ROWS, WIDTH), F32)
    for block in range(2):
        mask = inside(size_of(place_ref, size_ref, block), first_row, (ROWS, WIDTH))
        own = jnp.where(mask, start_ref[block, pl.ds(first_row, ROWS)].astype(F32), 0.0)
        rows_ref[block] = own
        square = own * own
        norm = norm + square
        diagonal = diagonal_of(
            left_levels_ref[block : block + 1], right_levels_ref[block : block + 1], first_row
        )
        diagonal_ref[block] = diagonal
        energy = energy + diagonal * square
    scalar_ref[...] = lanes([total(energy), total(norm)], LANES)
    before_ref[:ROWS] = rows_ref[0]
    place = lax.broadcasted_iota(jnp.int32, (8, WIDTH), 0)
    before_ref[ROWS:] = jnp.where(
        place == 0, left_levels_ref[0:1], jnp.where(place == 1, right_levels_ref[0:1], 0.0)
    )


def mask_kernel(place_ref, size_ref, start_ref, halo_ref, field_ref):
    core = place_ref[0]

    def masked(source, block):
        mask = inside(size_of(place_ref, size_ref, block), 0, (WIDTH, WIDTH))
        return jnp.where(mask, source.astype(F32), 0.0).astype(BF16)

    field_ref[0] = masked(start_ref[core], core)

    @pl.when(core == 0)
    def _():
        field_ref[1] = masked(start_ref[1], 1)

    @pl.when(core == 1)
    def _():
        field_ref[1] = masked(halo_ref[...], 2)


def images(place_ref, spin_ref, left_ref, right_ref, other_ref, field, after):
    core = place_ref[0]
    here = place_ref[2] + core
    following = jnp.minimum(here + 1, spin_ref.shape[0] - 1)
    above = jnp.full((1, WIDTH), spin_ref[following], jnp.int32).astype(F32) + 1.0
    below = jnp.full((1, WIDTH), spin_ref[here], jnp.int32).astype(F32) + 1.0
    linked = jnp.full((1, WIDTH), here, jnp.int32) + 1 < spin_ref.shape[0]
    coupling = jnp.where(linked, jnp.sqrt(above / below), 0.0)
    lowered = raised = None
    for left, right in (
        (left_ref[0, core], right_ref[0, core]),
        (other_ref[0], other_ref[1]),
    ):
        up = product(left, product(field, right, 1).astype(BF16))
        down = product(product(left.T, after).astype(BF16), right)
        raised = up if raised is None else raised + up
        lowered = down if lowered is None else lowered + down
    return coupling * lowered, coupling * raised


def put_parts(lowered, raised, after, scalars, parts_ref):
    energy = 2.0 * total(raised * after.astype(F32))
    row = lanes([energy], LANES) + scalars
    high = row.astype(BF16).astype(F32)
    middle = (row - high).astype(BF16).astype(F32)
    low = (row - high) - middle
    place = lax.broadcasted_iota(jnp.int32, (16, LANES), 0)
    coded = jnp.where(
        place == 0, high, jnp.where(place == 1, middle, jnp.where(place == 2, low, 0.0))
    ).astype(BF16)
    for device in range(NOP):
        here = slice(device * ROWS, (device + 1) * ROWS)
        for index, image in enumerate((lowered, raised)):
            rounded = image[here].astype(BF16)
            for tile in range(TILES):
                there = (index * TILES + tile) * ROWS
                columns = slice(tile * LANES, (tile + 1) * LANES)
                parts_ref[device, there : there + ROWS] = rounded[:, columns]
        parts_ref[device, 2 * ROWS * TILES :] = coded


def first_kernel(
    place_ref, spin_ref, field_ref, scalar_ref, left_ref, right_ref, other_ref, parts_ref
):
    after = field_ref[1]
    lowered, raised = images(
        place_ref, spin_ref, left_ref, right_ref, other_ref, field_ref[0], after
    )
    put_parts(lowered, raised, after, scalar_ref[...], parts_ref)


def second_kernel(
    place_ref, spin_ref, gathered_ref, scalar_ref, left_ref, right_ref, other_ref, parts_ref
):
    field = gathered_ref[:, :ROWS].reshape(WIDTH, WIDTH)
    after = gathered_ref[:, ROWS:].reshape(WIDTH, WIDTH)
    lowered, raised = images(place_ref, spin_ref, left_ref, right_ref, other_ref, field, after)
    put_parts(lowered, raised, after, scalar_ref[...], parts_ref)


def sum_kernel(
    received_ref, first_ref, second_ref, first_sent_ref, leaving_sent_ref, scalar_ref
):
    coded = jnp.zeros((16, LANES), F32)
    for device in range(NOP):
        coded = coded + received_ref[device, 2 * ROWS * TILES :].astype(F32)
    row = jnp.concatenate([jnp.sum(coded, axis=0, keepdims=True)] * 2, axis=1)
    scalar_ref[...] = jnp.broadcast_to(row[None], scalar_ref.shape)
    for tile in range(TILES):
        sums = [jnp.zeros((ROWS, LANES), F32) for _ in range(BLOCKS)]
        for device in range(NOP):
            for index in range(2):
                there = (index * TILES + tile) * ROWS
                block = device % 2 + index
                sums[block] = sums[block] + received_ref[device, there : there + ROWS].astype(F32)
        columns = slice(tile * LANES, (tile + 1) * LANES)
        first_ref[:, columns] = sums[0]
        second_ref[:, columns] = sums[1]
        first_sent_ref[:, columns] = sums[0].astype(BF16)
        leaving_sent_ref[:, columns] = sums[2].astype(BF16)


def scalars_of(gathered_ref, count):
    row = jnp.sum(gathered_ref[...], axis=0)
    return [row[:, index : index + 1] for index in range(count)]


def correction_kernel(
    place_ref, size_ref, gathered_ref, first_ref, second_ref, leaving_ref, arrived_ref,
    ahead_ref, diagonal_ref, rows_ref, beyond_ref,
    spread_ref, image_ref, change_ref, scalar_ref, known_ref,
):
    energy, norm = scalars_of(gathered_ref, 2)
    rayleigh = energy / norm
    scale = jnp.sqrt(norm)
    first_row = own_rows(place_ref)
    sums = [
        first_ref[...].astype(F32) + arrived_ref[...].astype(F32),
        second_ref[...],
        leaving_ref[...].astype(F32) + ahead_ref[...].astype(F32),
    ]
    amounts = [jnp.zeros((ROWS, WIDTH), F32) for _ in range(4)]
    for block in range(BLOCKS):
        mask = inside(size_of(place_ref, size_ref, block), first_row, (ROWS, WIDTH))
        if block == 2:
            values = beyond_ref[:ROWS]
            diagonal = diagonal_of(
                beyond_ref[ROWS : ROWS + 1], beyond_ref[ROWS + 1 : ROWS + 2], first_row
            )
        else:
            values = rows_ref[block]
            diagonal = diagonal_ref[block]
        unit = values / scale
        image = jnp.where(mask, sums[block] + diagonal * values, 0.0) / scale
        residual = image - rayleigh * unit
        change = residual / (jnp.abs(diagonal - rayleigh) + 1.0)
        rounded = change.astype(BF16)
        for device in range(NOP):
            part = block - device % 2
            if part in (0, 1):
                spread_ref[device, part * ROWS : (part + 1) * ROWS] = rounded
        if block < 2:
            image_ref[block] = image
            change_ref[block] = change
            again = rounded.astype(F32)
            amounts[0] = amounts[0] + diagonal * again * again
            amounts[1] = amounts[1] + unit * change
            amounts[2] = amounts[2] + change * change
            amounts[3] = amounts[3] + change * image
    scalar_ref[...] = lanes([total(amount) for amount in amounts], LANES)
    known_ref[...] = lanes([rayleigh, scale], LANES)


def ritz_kernel(
    place_ref, size_ref, gathered_ref, known_ref, first_ref, second_ref, arrived_ref,
    diagonal_ref, rows_ref, image_ref, change_ref,
    vector_ref, residual_ref, energies_ref,
):
    change_energy, correlation, square, change_image = scalars_of(gathered_ref, 4)
    rayleigh = known_ref[:, 0:1]
    scale = known_ref[:, 1:2]
    spread = square - correlation * correlation
    deviation = jnp.sqrt(spread)
    cross_term = (change_image - correlation * rayleigh) / deviation
    second_energy = (
        change_energy - 2.0 * correlation * change_image + correlation * correlation * rayleigh
    ) / spread
    half_gap = 0.5 * (rayleigh - second_energy)
    length = jnp.sqrt(half_gap * half_gap + cross_term * cross_term)
    lowest = 0.5 * (rayleigh + second_energy) - length
    apart = length > 0.0
    divisor = jnp.where(apart, length, 1.0)
    double_cosine = jnp.where(apart, half_gap / divisor, 1.0)
    double_sine = jnp.where(apart, cross_term / divisor, 0.0)
    larger = jnp.sqrt(0.5 * (1.0 + jnp.abs(double_cosine)))
    smaller = 0.5 * double_sine / larger
    ahead = double_cosine >= 0.0
    sign = jnp.where(cross_term < 0.0, -1.0, 1.0)
    cosine_angle = jnp.where(ahead, larger, jnp.abs(smaller))
    sine_angle = jnp.where(ahead, smaller, sign * larger)
    first_row = own_rows(place_ref)
    sums = [first_ref[...] + arrived_ref[...].astype(F32), second_ref[...]]
    for block in range(2):
        mask = inside(size_of(place_ref, size_ref, block), first_row, (ROWS, WIDTH))
        unit = rows_ref[block] / scale
        image = image_ref[block]
        change = change_ref[block]
        rounded = change.astype(BF16).astype(F32)
        change_picture = jnp.where(mask, sums[block] + diagonal_ref[block] * rounded, 0.0)
        unit_second = (change - correlation * unit) / deviation
        second_image = (change_picture - correlation * image) / deviation
        ritz_unit = sine_angle * unit - cosine_angle * unit_second
        vector_ref[block] = (scale * ritz_unit).astype(BF16)
        residual_ref[block] = (
            scale * (sine_angle * image - cosine_angle * second_image - lowest * ritz_unit)
        ).astype(BF16)
    energies_ref[...] = lanes([rayleigh, lowest], 2)


def line(distance):
    devices = range(lax.axis_size(SEC))
    return [(i, i + distance) for i in devices if i + distance in devices]


def body(start, left, right, left_energy, right_energy, sector_size, sector_spin):
    core = lax.axis_index("c")
    position = lax.axis_index(OP)
    sectors = lax.axis_size(SEC)
    place = jnp.stack([core, position, 2 * lax.axis_index(SEC)]).astype(jnp.int32)
    block_shape = shaped((WIDTH, WIDTH), BF16)
    two_shape = shaped((2, WIDTH, WIDTH), BF16)
    own_shape = shaped((2, ROWS, WIDTH), F32)
    row_shape = shaped((ROWS, WIDTH), F32)
    lane_shape = shaped((1, LANES), F32)
    parts_shape = shaped((NOP, PART, LANES), BF16)
    work = 16 * WIDTH * WIDTH * WIDTH

    halo_source, send = call(
        open_kernel, (block_shape, two_shape), [HBM] * 3, [pltpu.SemaphoreType.DMA((3,))],
        vmem=WHOLE_VMEM,
    )(start, left, right)
    to_second_core = [(sectors + i + 1, sectors + i) for i in range(sectors - 1)]
    halo = lax.ppermute(halo_source, ("c",) + SEC, to_second_core)
    other = lax.ppermute(send, "c", [(0, 1), (1, 0)])
    rows, diagonal, amounts, before = call(
        rows_kernel,
        (own_shape, own_shape, lane_shape, shaped((ROWS + 8, WIDTH), F32)),
        [SM] * 2 + [VM] * 3,
    )(place, sector_size, start, left_energy, right_energy)
    beyond = lax.ppermute(before, SEC, line(-1))
    field = call(mask_kernel, two_shape, [SM] * 2 + [VM] * 2, flops=4 * work)(
        place, sector_size, start, halo
    )

    def summed(received):
        sent_shape = shaped((ROWS, WIDTH), BF16)
        scalar_shape = shaped((sectors, 1, 2 * LANES), F32)
        *sums, scalars = call(
            sum_kernel, (row_shape,) * 2 + (sent_shape,) * 2 + (scalar_shape,), [VM]
        )(received)
        return (*sums, lax.all_to_all(scalars, SEC, 0, 0))

    parts = call(first_kernel, parts_shape, [SM] * 2 + [VM] * 5, flops=work, nbytes=4 << 20)(
        place, sector_spin, field, amounts, left, right, other
    )
    received = lax.all_to_all(parts, OP, 0, 0)
    received, beyond = lax.optimization_barrier((received, beyond))
    first, second, first_sent, leaving_sent, gathered = summed(received)
    arrived = lax.ppermute(leaving_sent, SEC, line(1))
    ahead = lax.ppermute(first_sent, SEC, line(-1))
    spread, image, change, amounts, known = call(
        correction_kernel,
        (shaped((NOP, 2 * ROWS, WIDTH), BF16), own_shape, own_shape, lane_shape, lane_shape),
        [SM] * 2 + [VM] * 9,
    )(
        place, sector_size, gathered, first_sent, second, leaving_sent, arrived, ahead,
        diagonal, rows, beyond,
    )
    fields = lax.all_to_all(spread, OP, 0, 0)
    parts = call(second_kernel, parts_shape, [SM] * 2 + [VM] * 5, flops=work, nbytes=4 << 20)(
        place, sector_spin, fields, amounts, left, right, other
    )
    first, second, first_sent, leaving_sent, gathered = summed(lax.all_to_all(parts, OP, 0, 0))
    arrived = lax.ppermute(leaving_sent, SEC, line(1))
    result = shaped((2, ROWS, WIDTH), BF16)
    vector, residual, energies = call(
        ritz_kernel, (result, result, shaped((1, 2), F32)), [SM] * 2 + [VM] * 9
    )(
        place, sector_size, gathered, known, first, second, arrived,
        diagonal, rows, image, change,
    )
    return vector, residual, energies.reshape(2)


def solution(mesh):
    fine = Mesh(mesh.devices.reshape(2, 4, 2, 2, 16), ("yh", "x", "c", "yl", "z"))
    return jax.shard_map(
        body,
        mesh=fine,
        in_specs=(
            P(SEC, None, None),
            P(OP, SEC, None, None),
            P(OP, SEC, None, None),
            P(SEC, None),
            P(SEC, None),
            P(),
            P(),
        ),
        out_specs=(P(SEC, OP, None), P(SEC, OP, None), P()),
        check_vma=False,
    )
```

```python
import jax
import jax.numpy as jnp
from jax import lax
from jax.experimental import pallas as pl
from jax.experimental.pallas import tpu as pltpu
from jax.sharding import Mesh, PartitionSpec as P

F32 = jnp.float32
BF16 = jnp.bfloat16
OP = ("yh", "x", "c")
SEC = ("yl", "z")
WIDTH = 512
ROWS = 32
NOP = 16
LANES = 128
TILES = WIDTH // LANES
PART = ROWS * TILES + 16
VMEM_LIMIT = 24 * 1024 * 1024
WHOLE_VMEM = 62 * 1024 * 1024

VM = pl.BlockSpec(memory_space=pltpu.VMEM)
SM = pl.BlockSpec(memory_space=pltpu.SMEM)
HBM = pl.BlockSpec(memory_space=pltpu.HBM)


def call(
    kernel, out_shape, in_specs, scratch=(), flops=0, nbytes=1 << 20, vmem=VMEM_LIMIT
):
    return pl.pallas_call(
        kernel,
        out_shape=out_shape,
        in_specs=in_specs,
        out_specs=jax.tree.map(lambda _: VM, out_shape),
        scratch_shapes=list(scratch),
        compiler_params=pltpu.CompilerParams(vmem_limit_bytes=vmem),
        cost_estimate=pl.CostEstimate(flops=flops, bytes_accessed=nbytes, transcendentals=0),
    )


def shaped(shape, dtype):
    return jax.ShapeDtypeStruct(shape, dtype)


def product(first, second, second_axis=0):
    return lax.dot_general(
        first, second, (((1,), (second_axis,)), ((), ())), preferred_element_type=F32
    )


def total(array):
    return jnp.sum(jnp.sum(array, axis=0, keepdims=True), axis=1, keepdims=True)


def lanes(values, width):
    place = lax.broadcasted_iota(jnp.int32, (1, width), 1)
    row = jnp.zeros((1, width), F32)
    for index, value in enumerate(values):
        row = jnp.where(place == index, value, row)
    return row


def three_parts(row):
    high = row.astype(BF16).astype(F32)
    middle = (row - high).astype(BF16).astype(F32)
    return high, middle, (row - high) - middle


def stacked(rows, count, width):
    place = lax.broadcasted_iota(jnp.int32, (count, width), 0)
    block = jnp.zeros((count, width), F32)
    for index, row in enumerate(rows):
        block = jnp.where(place == index, row, block)
    return block.astype(BF16)


def own_rows(place_ref):
    return pl.multiple_of(place_ref[1] * ROWS, ROWS)


def inside(size, first_row, shape):
    rows = lax.broadcasted_iota(jnp.int32, shape, 0) + first_row
    columns = lax.broadcasted_iota(jnp.int32, shape, 1)
    return (rows < size) & (columns < size)


def size_of(place_ref, size_ref, block):
    return size_ref[jnp.minimum(place_ref[2] + block, size_ref.shape[0] - 1)]


def diagonal_of(left_row, right_row, first_row):
    rows = lax.broadcasted_iota(jnp.int32, (ROWS, WIDTH), 0) + first_row
    columns = lax.broadcasted_iota(jnp.int32, (ROWS, WIDTH), 1)
    chosen = jnp.where(rows == columns, left_row, 0.0)
    return jnp.sum(chosen, axis=1, keepdims=True) + right_row


def open_kernel(start_ref, left_ref, right_ref, halo_ref, send_ref, semaphores):
    there = 1 - lax.axis_index("c")
    copies = [
        pltpu.make_async_copy(start_ref.at[0], halo_ref, semaphores.at[0]),
        pltpu.make_async_copy(left_ref.at[0, there], send_ref.at[0], semaphores.at[1]),
        pltpu.make_async_copy(right_ref.at[0, there], send_ref.at[1], semaphores.at[2]),
    ]
    for copy in copies:
        copy.start()
    for copy in copies:
        copy.wait()


def rows_kernel(
    place_ref, size_ref, start_ref, left_levels_ref, right_levels_ref,
    rows_ref, diagonal_ref, scalar_ref,
):
    first_row = own_rows(place_ref)
    norm = jnp.zeros((ROWS, WIDTH), F32)
    energy = jnp.zeros((ROWS, WIDTH), F32)
    for block in range(2):
        mask = inside(size_of(place_ref, size_ref, block), first_row, (ROWS, WIDTH))
        own = jnp.where(mask, start_ref[block, pl.ds(first_row, ROWS)].astype(F32), 0.0)
        rows_ref[block] = own
        square = own * own
        norm = norm + square
        diagonal = diagonal_of(
            left_levels_ref[block : block + 1], right_levels_ref[block : block + 1], first_row
        )
        diagonal_ref[block] = diagonal
        energy = energy + diagonal * square
    scalar_ref[...] = lanes([total(energy), total(norm)], LANES)


def masked(source, place_ref, size_ref, block):
    mask = inside(size_of(place_ref, size_ref, block), 0, (WIDTH, WIDTH))
    return jnp.where(mask, source.astype(F32), 0.0).astype(BF16)


def coupling_of(place_ref, spin_ref):
    here = place_ref[2] + place_ref[0]
    following = jnp.minimum(here + 1, spin_ref.shape[0] - 1)
    above = jnp.full((1, WIDTH), spin_ref[following], jnp.int32).astype(F32) + 1.0
    below = jnp.full((1, WIDTH), spin_ref[here], jnp.int32).astype(F32) + 1.0
    linked = jnp.full((1, WIDTH), here, jnp.int32) + 1 < spin_ref.shape[0]
    return jnp.where(linked, jnp.sqrt(above / below), 0.0)


def operator_pairs(place_ref, left_ref, right_ref, other_ref):
    core = place_ref[0]
    return (left_ref[0, core], right_ref[0, core]), (other_ref[0], other_ref[1])


def raise_into(place_ref, spin_ref, left_ref, right_ref, other_ref, field, raised_ref):
    image = jnp.zeros((WIDTH, WIDTH), F32)
    for left, right in operator_pairs(place_ref, left_ref, right_ref, other_ref):
        image = image + product(left, product(field, right, 1).astype(BF16))
    raised_ref[...] = (coupling_of(place_ref, spin_ref) * image).astype(BF16)


def lower_into(
    place_ref, spin_ref, left_ref, right_ref, other_ref, after, raised_ref, scalars,
    lowered_ref, scalar_ref,
):
    image = jnp.zeros((WIDTH, WIDTH), F32)
    for left, right in operator_pairs(place_ref, left_ref, right_ref, other_ref):
        image = image + product(product(left.T, after).astype(BF16), right)
    lowered_ref[...] = coupling_of(place_ref, spin_ref) * image
    energy = 2.0 * total(raised_ref[...].astype(F32) * after.astype(F32))
    scalar_ref[...] = lanes([energy], LANES) + scalars


def first_raise_kernel(
    place_ref, size_ref, spin_ref, start_ref, left_ref, right_ref, other_ref, raised_ref
):
    core = place_ref[0]
    field = masked(start_ref[core], place_ref, size_ref, core)
    raise_into(place_ref, spin_ref, left_ref, right_ref, other_ref, field, raised_ref)


def first_lower_kernel(
    place_ref, size_ref, spin_ref, start_ref, halo_ref, raised_ref, known_ref,
    left_ref, right_ref, other_ref, lowered_ref, scalar_ref,
):
    core = place_ref[0]
    source = jnp.where(core == 0, start_ref[1].astype(F32), halo_ref[...].astype(F32))
    after = masked(source, place_ref, size_ref, core + 1)
    lower_into(
        place_ref, spin_ref, left_ref, right_ref, other_ref, after, raised_ref, known_ref[...],
        lowered_ref, scalar_ref,
    )


def second_raise_kernel(
    place_ref, spin_ref, gathered_ref, left_ref, right_ref, other_ref, raised_ref
):
    field = gathered_ref[...].reshape(WIDTH, WIDTH)
    raise_into(place_ref, spin_ref, left_ref, right_ref, other_ref, field, raised_ref)


def second_lower_kernel(
    place_ref, spin_ref, after_ref, raised_ref, known_ref, left_ref, right_ref, other_ref,
    lowered_ref, scalar_ref,
):
    after = after_ref[...].reshape(WIDTH, WIDTH)
    lower_into(
        place_ref, spin_ref, left_ref, right_ref, other_ref, after, raised_ref, known_ref[...],
        lowered_ref, scalar_ref,
    )


def parts_kernel(lowered_ref, arrived_ref, scalar_ref, parts_ref):
    coded = stacked(three_parts(scalar_ref[...]), 16, LANES)
    for device in range(NOP):
        here = slice(device * ROWS, (device + 1) * ROWS)
        image = (lowered_ref[here] + arrived_ref[here].astype(F32)).astype(BF16)
        for tile in range(TILES):
            columns = slice(tile * LANES, (tile + 1) * LANES)
            parts_ref[device, tile * ROWS : (tile + 1) * ROWS] = image[:, columns]
        parts_ref[device, ROWS * TILES :] = coded


def sum_kernel(received_ref, sums_ref, scalar_ref):
    coded = jnp.zeros((16, LANES), F32)
    for device in range(NOP):
        coded = coded + received_ref[device, ROWS * TILES :].astype(F32)
    row = jnp.sum(coded, axis=0, keepdims=True)
    scalar_ref[...] = jnp.broadcast_to(row[None], scalar_ref.shape)
    for block in range(2):
        for tile in range(TILES):
            running = jnp.zeros((ROWS, LANES), F32)
            for device in range(block, NOP, 2):
                here = slice(tile * ROWS, (tile + 1) * ROWS)
                running = running + received_ref[device, here].astype(F32)
            sums_ref[block, :, tile * LANES : (tile + 1) * LANES] = running


def scalars_of(gathered_ref, count):
    row = jnp.sum(gathered_ref[...], axis=0)
    return [row[:, index : index + 1] for index in range(count)]


def correction_kernel(
    place_ref, size_ref, gathered_ref, sums_ref, diagonal_ref, rows_ref,
    spread_ref, image_ref, change_ref, scalar_ref, known_ref,
):
    energy, norm = scalars_of(gathered_ref, 2)
    rayleigh = energy / norm
    scale = jnp.sqrt(norm)
    first_row = own_rows(place_ref)
    amounts = [jnp.zeros((ROWS, WIDTH), F32) for _ in range(4)]
    for block in range(2):
        mask = inside(size_of(place_ref, size_ref, block), first_row, (ROWS, WIDTH))
        values = rows_ref[block]
        diagonal = diagonal_ref[block]
        unit = values / scale
        image = jnp.where(mask, sums_ref[block] + diagonal * values, 0.0) / scale
        residual = image - rayleigh * unit
        change = residual / (jnp.abs(diagonal - rayleigh) + 1.0)
        rounded = change.astype(BF16)
        for device in range(block, NOP, 2):
            spread_ref[device] = rounded
        image_ref[block] = image
        change_ref[block] = change
        again = rounded.astype(F32)
        amounts[0] = amounts[0] + diagonal * again * again
        amounts[1] = amounts[1] + unit * change
        amounts[2] = amounts[2] + change * change
        amounts[3] = amounts[3] + change * image
    scalar_ref[...] = lanes([total(amount) for amount in amounts], LANES)
    known_ref[...] = lanes([rayleigh, scale], LANES)


def ritz_kernel(
    place_ref, size_ref, gathered_ref, known_ref, sums_ref,
    diagonal_ref, rows_ref, image_ref, change_ref,
    vector_ref, residual_ref, energies_ref,
):
    change_energy, correlation, square, change_image = scalars_of(gathered_ref, 4)
    rayleigh = known_ref[:, 0:1]
    scale = known_ref[:, 1:2]
    spread = square - correlation * correlation
    deviation = jnp.sqrt(spread)
    cross_term = (change_image - correlation * rayleigh) / deviation
    second_energy = (
        change_energy - 2.0 * correlation * change_image + correlation * correlation * rayleigh
    ) / spread
    half_gap = 0.5 * (rayleigh - second_energy)
    length = jnp.sqrt(half_gap * half_gap + cross_term * cross_term)
    lowest = 0.5 * (rayleigh + second_energy) - length
    apart = length > 0.0
    divisor = jnp.where(apart, length, 1.0)
    double_cosine = jnp.where(apart, half_gap / divisor, 1.0)
    double_sine = jnp.where(apart, cross_term / divisor, 0.0)
    larger = jnp.sqrt(0.5 * (1.0 + jnp.abs(double_cosine)))
    smaller = 0.5 * double_sine / larger
    ahead = double_cosine >= 0.0
    sign = jnp.where(cross_term < 0.0, -1.0, 1.0)
    cosine_angle = jnp.where(ahead, larger, jnp.abs(smaller))
    sine_angle = jnp.where(ahead, smaller, sign * larger)
    first_row = own_rows(place_ref)
    for block in range(2):
        mask = inside(size_of(place_ref, size_ref, block), first_row, (ROWS, WIDTH))
        unit = rows_ref[block] / scale
        image = image_ref[block]
        change = change_ref[block]
        rounded = change.astype(BF16).astype(F32)
        change_picture = jnp.where(mask, sums_ref[block] + diagonal_ref[block] * rounded, 0.0)
        unit_second = (change - correlation * unit) / deviation
        second_image = (change_picture - correlation * image) / deviation
        ritz_unit = sine_angle * unit - cosine_angle * unit_second
        vector_ref[block] = (scale * ritz_unit).astype(BF16)
        residual_ref[block] = (
            scale * (sine_angle * image - cosine_angle * second_image - lowest * ritz_unit)
        ).astype(BF16)
    energies_ref[...] = lanes([rayleigh, lowest], 2)


def body(start, left, right, left_energy, right_energy, sector_size, sector_spin):
    core = lax.axis_index("c")
    position = lax.axis_index(OP)
    sectors = lax.axis_size(SEC)
    place = jnp.stack([core, position, 2 * lax.axis_index(SEC)]).astype(jnp.int32)
    block_shape = shaped((WIDTH, WIDTH), BF16)
    two_shape = shaped((2, WIDTH, WIDTH), BF16)
    own_shape = shaped((2, ROWS, WIDTH), F32)
    lane_shape = shaped((1, LANES), F32)
    work = 8 * WIDTH * WIDTH * WIDTH
    owners = ("c",) + SEC
    within = [(i, sectors + i) for i in range(sectors)]
    across = [(sectors + i, i + 1) for i in range(sectors - 1)]
    to_next = within + across
    to_previous = [(there, here) for here, there in to_next]

    halo_source, send = call(
        open_kernel, (block_shape, two_shape), [HBM] * 3, [pltpu.SemaphoreType.DMA((3,))],
        vmem=WHOLE_VMEM,
    )(start, left, right)
    other = lax.ppermute(send, "c", [(0, 1), (1, 0)])
    halo = lax.ppermute(halo_source, owners, [(there, here) for here, there in across])
    operators = (left, right, other)
    rows, diagonal, amounts = call(
        rows_kernel, (own_shape, own_shape, lane_shape), [SM] * 2 + [VM] * 3
    )(place, sector_size, start, left_energy, right_energy)

    def summed(lowered, raised, amounts):
        arrived = lax.ppermute(raised, owners, to_next)
        parts = call(parts_kernel, shaped((NOP, PART, LANES), BF16), [VM] * 3)(
            lowered, arrived, amounts
        )
        sums, scalars = call(sum_kernel, (own_shape, shaped((sectors, 1, LANES), F32)), [VM])(
            lax.all_to_all(parts, OP, 0, 0)
        )
        return sums, lax.all_to_all(scalars, SEC, 0, 0)

    lowered_shapes = (shaped((WIDTH, WIDTH), F32), lane_shape)
    raised = call(
        first_raise_kernel, block_shape, [SM] * 3 + [VM] * 4, flops=work, nbytes=4 << 20
    )(place, sector_size, sector_spin, start, *operators)
    lowered, amounts = call(
        first_lower_kernel, lowered_shapes, [SM] * 3 + [VM] * 7, flops=work, nbytes=4 << 20
    )(place, sector_size, sector_spin, start, halo, raised, amounts, *operators)
    sums, gathered = summed(lowered, raised, amounts)
    spread, image, change, amounts, known = call(
        correction_kernel,
        (shaped((NOP, ROWS, WIDTH), BF16), own_shape, own_shape, lane_shape, lane_shape),
        [SM] * 2 + [VM] * 4,
    )(place, sector_size, gathered, sums, diagonal, rows)
    field = lax.all_to_all(spread, OP, 0, 0)
    after = lax.ppermute(field, owners, to_previous)
    raised = call(
        second_raise_kernel, block_shape, [SM] * 2 + [VM] * 4, flops=work, nbytes=4 << 20
    )(place, sector_spin, field, *operators)
    lowered, amounts = call(
        second_lower_kernel, lowered_shapes, [SM] * 2 + [VM] * 6, flops=work, nbytes=4 << 20
    )(place, sector_spin, after, raised, amounts, *operators)
    sums, gathered = summed(lowered, raised, amounts)
    result = shaped((2, ROWS, WIDTH), BF16)
    vector, residual, energies = call(
        ritz_kernel, (result, result, shaped((1, 2), F32)), [SM] * 2 + [VM] * 7
    )(place, sector_size, gathered, known, sums, diagonal, rows, image, change)
    return vector, residual, energies.reshape(2)


def solution(mesh):
    fine = Mesh(mesh.devices.reshape(2, 4, 2, 2, 16), ("yh", "x", "c", "yl", "z"))
    return jax.shard_map(
        body,
        mesh=fine,
        in_specs=(
            P(SEC, None, None),
            P(OP, SEC, None, None),
            P(OP, SEC, None, None),
            P(SEC, None),
            P(SEC, None),
            P(),
            P(),
        ),
        out_specs=(P(SEC, OP, None), P(SEC, OP, None), P()),
        check_vma=False,
    )
```

```python
import jax
import jax.numpy as jnp
from jax import lax
from jax.experimental import pallas as pl
from jax.experimental.pallas import tpu as pltpu
from jax.sharding import Mesh, PartitionSpec as P

F32 = jnp.float32
BF16 = jnp.bfloat16
OP = ("yh", "x", "c")
SEC = ("yl", "z")
WIDTH = 512
ROWS = 32
NOP = 16
LANES = 128
TILES = WIDTH // LANES
PART = ROWS * TILES + 16
VMEM_LIMIT = 24 * 1024 * 1024
WHOLE_VMEM = 62 * 1024 * 1024

VM = pl.BlockSpec(memory_space=pltpu.VMEM)
SM = pl.BlockSpec(memory_space=pltpu.SMEM)
HBM = pl.BlockSpec(memory_space=pltpu.HBM)


def call(
    kernel, out_shape, in_specs, scratch=(), flops=0, nbytes=1 << 20, vmem=VMEM_LIMIT
):
    return pl.pallas_call(
        kernel,
        out_shape=out_shape,
        in_specs=in_specs,
        out_specs=jax.tree.map(lambda _: VM, out_shape),
        scratch_shapes=list(scratch),
        compiler_params=pltpu.CompilerParams(vmem_limit_bytes=vmem),
        cost_estimate=pl.CostEstimate(flops=flops, bytes_accessed=nbytes, transcendentals=0),
    )


def shaped(shape, dtype):
    return jax.ShapeDtypeStruct(shape, dtype)


def product(first, second, second_axis=0):
    return lax.dot_general(
        first, second, (((1,), (second_axis,)), ((), ())), preferred_element_type=F32
    )


def total(array):
    return jnp.sum(jnp.sum(array, axis=0, keepdims=True), axis=1, keepdims=True)


def lanes(values, width):
    place = lax.broadcasted_iota(jnp.int32, (1, width), 1)
    row = jnp.zeros((1, width), F32)
    for index, value in enumerate(values):
        row = jnp.where(place == index, value if value.shape[1] == 1 else value[:, :width], row)
    return row


def three_parts(row):
    high = row.astype(BF16).astype(F32)
    middle = (row - high).astype(BF16).astype(F32)
    return high, middle, (row - high) - middle


def stacked(rows, count, width):
    place = lax.broadcasted_iota(jnp.int32, (count, width), 0)
    block = jnp.zeros((count, width), F32)
    for index, row in enumerate(rows):
        block = jnp.where(place == index, row, block)
    return block.astype(BF16)


def own_rows(place_ref):
    return pl.multiple_of(place_ref[1] * ROWS, ROWS)


def inside(size, first_row, shape):
    rows = lax.broadcasted_iota(jnp.int32, shape, 0) + first_row
    columns = lax.broadcasted_iota(jnp.int32, shape, 1)
    return (rows < size) & (columns < size)


def size_of(place_ref, size_ref, block):
    return size_ref[jnp.minimum(place_ref[2] + block, size_ref.shape[0] - 1)]


def diagonal_of(left_row, right_row, first_row):
    rows = lax.broadcasted_iota(jnp.int32, (ROWS, WIDTH), 0) + first_row
    columns = lax.broadcasted_iota(jnp.int32, (ROWS, WIDTH), 1)
    chosen = jnp.where(rows == columns, left_row, 0.0)
    return jnp.sum(chosen, axis=1, keepdims=True) + right_row


def open_kernel(start_ref, left_ref, right_ref, halo_ref, send_ref, own_ref, semaphores):
    core = lax.axis_index("c")
    copies = [
        pltpu.make_async_copy(source, target, semaphores.at[index])
        for index, (source, target) in enumerate(
            (
                (left_ref.at[0, 1 - core], send_ref.at[0]),
                (right_ref.at[0, 1 - core], send_ref.at[1]),
                (start_ref.at[0], halo_ref),
                (left_ref.at[0, core], own_ref.at[0]),
                (right_ref.at[0, core], own_ref.at[1]),
                (start_ref.at[core], own_ref.at[2]),
            )
        )
    ]
    for copy in copies:
        copy.start()
    for copy in copies:
        copy.wait()


def rows_kernel(
    place_ref, size_ref, start_ref, left_levels_ref, right_levels_ref,
    rows_ref, diagonal_ref, scalar_ref,
):
    first_row = own_rows(place_ref)
    norm = jnp.zeros((ROWS, WIDTH), F32)
    energy = jnp.zeros((ROWS, WIDTH), F32)
    for block in range(2):
        mask = inside(size_of(place_ref, size_ref, block), first_row, (ROWS, WIDTH))
        own = jnp.where(mask, start_ref[block, pl.ds(first_row, ROWS)].astype(F32), 0.0)
        rows_ref[block] = own
        square = own * own
        norm = norm + square
        diagonal = diagonal_of(
            left_levels_ref[block : block + 1], right_levels_ref[block : block + 1], first_row
        )
        diagonal_ref[block] = diagonal
        energy = energy + diagonal * square
    scalar_ref[...] = lanes([total(energy), total(norm)], LANES)


def masked(source, place_ref, size_ref, block):
    mask = inside(size_of(place_ref, size_ref, block), 0, (WIDTH, WIDTH))
    return jnp.where(mask, source.astype(F32), 0.0).astype(BF16)


def coupling_of(place_ref, spin_ref):
    here = place_ref[2] + place_ref[0]
    following = jnp.minimum(here + 1, spin_ref.shape[0] - 1)
    above = jnp.full((1, WIDTH), spin_ref[following], jnp.int32).astype(F32) + 1.0
    below = jnp.full((1, WIDTH), spin_ref[here], jnp.int32).astype(F32) + 1.0
    linked = jnp.full((1, WIDTH), here, jnp.int32) + 1 < spin_ref.shape[0]
    return jnp.where(linked, jnp.sqrt(above / below), 0.0)


def operator_pairs(own_ref, other_ref):
    return (own_ref[0], own_ref[1]), (other_ref[0], other_ref[1])


def raise_into(place_ref, spin_ref, own_ref, other_ref, field, raised_ref):
    image = jnp.zeros((WIDTH, WIDTH), F32)
    for left, right in operator_pairs(own_ref, other_ref):
        image = image + product(left, product(field, right, 1).astype(BF16))
    raised_ref[...] = (coupling_of(place_ref, spin_ref) * image).astype(BF16)


def lower_into(
    place_ref, spin_ref, own_ref, other_ref, after, raised_ref, scalars,
    lowered_ref, scalar_ref,
):
    image = jnp.zeros((WIDTH, WIDTH), F32)
    for left, right in operator_pairs(own_ref, other_ref):
        image = image + product(product(left.T, after).astype(BF16), right)
    lowered_ref[...] = coupling_of(place_ref, spin_ref) * image
    energy = 2.0 * total(raised_ref[...].astype(F32) * after.astype(F32))
    scalar_ref[...] = lanes([energy], LANES) + scalars


def first_raise_kernel(
    place_ref, size_ref, spin_ref, own_ref, other_ref, raised_ref
):
    core = place_ref[0]
    field = masked(own_ref[2], place_ref, size_ref, core)
    raise_into(place_ref, spin_ref, own_ref, other_ref, field, raised_ref)


def first_lower_kernel(
    place_ref, size_ref, spin_ref, start_ref, halo_ref, raised_ref, known_ref,
    own_ref, other_ref, lowered_ref, scalar_ref,
):
    core = place_ref[0]
    source = jnp.where(core == 0, start_ref[1].astype(F32), halo_ref[...].astype(F32))
    after = masked(source, place_ref, size_ref, core + 1)
    lower_into(
        place_ref, spin_ref, own_ref, other_ref, after, raised_ref, known_ref[...],
        lowered_ref, scalar_ref,
    )


def second_raise_kernel(
    place_ref, spin_ref, gathered_ref, own_ref, other_ref, raised_ref
):
    field = gathered_ref[...].reshape(WIDTH, WIDTH)
    raise_into(place_ref, spin_ref, own_ref, other_ref, field, raised_ref)


def second_lower_kernel(
    place_ref, spin_ref, after_ref, raised_ref, known_ref, own_ref, other_ref,
    lowered_ref, scalar_ref,
):
    after = after_ref[...].reshape(WIDTH, WIDTH)
    lower_into(
        place_ref, spin_ref, own_ref, other_ref, after, raised_ref, known_ref[...],
        lowered_ref, scalar_ref,
    )


def parts_kernel(lowered_ref, arrived_ref, scalar_ref, parts_ref):
    coded = stacked(three_parts(scalar_ref[...]), 16, LANES)
    for device in range(NOP):
        here = slice(device * ROWS, (device + 1) * ROWS)
        image = (lowered_ref[here] + arrived_ref[here].astype(F32)).astype(BF16)
        for tile in range(TILES):
            columns = slice(tile * LANES, (tile + 1) * LANES)
            parts_ref[device, tile * ROWS : (tile + 1) * ROWS] = image[:, columns]
        parts_ref[device, ROWS * TILES :] = coded


def sum_kernel(received_ref, sums_ref, scalar_ref):
    coded = jnp.zeros((16, LANES), F32)
    for device in range(NOP):
        coded = coded + received_ref[device, ROWS * TILES :].astype(F32)
    row = jnp.sum(coded, axis=0, keepdims=True)
    scalar_ref[...] = jnp.broadcast_to(row[None], scalar_ref.shape)
    for block in range(2):
        for tile in range(TILES):
            running = jnp.zeros((ROWS, LANES), F32)
            for device in range(block, NOP, 2):
                here = slice(tile * ROWS, (tile + 1) * ROWS)
                running = running + received_ref[device, here].astype(F32)
            sums_ref[block, :, tile * LANES : (tile + 1) * LANES] = running


def widened(row, index):
    return jnp.broadcast_to(row[:, index : index + 1], (1, WIDTH))


def scalars_of(gathered_ref, count):
    row = jnp.sum(gathered_ref[...], axis=0)
    return [widened(row, index) for index in range(count)]


def correction_kernel(
    place_ref, size_ref, gathered_ref, sums_ref, diagonal_ref, rows_ref,
    spread_ref, image_ref, change_ref, scalar_ref, known_ref,
):
    energy, norm = scalars_of(gathered_ref, 2)
    rayleigh = energy / norm
    scale = jnp.sqrt(norm)
    shrink = 1.0 / scale
    first_row = own_rows(place_ref)
    amounts = [jnp.zeros((ROWS, WIDTH), F32) for _ in range(4)]
    for block in range(2):
        mask = inside(size_of(place_ref, size_ref, block), first_row, (ROWS, WIDTH))
        values = rows_ref[block]
        diagonal = diagonal_ref[block]
        unit = values * shrink
        image = jnp.where(mask, sums_ref[block] + diagonal * values, 0.0) * shrink
        residual = image - rayleigh * unit
        change = residual / (jnp.abs(diagonal - rayleigh) + 1.0)
        rounded = change.astype(BF16)
        for device in range(block, NOP, 2):
            spread_ref[device] = rounded
        image_ref[block] = image
        change_ref[block] = change
        again = rounded.astype(F32)
        amounts[0] = amounts[0] + diagonal * again * again
        amounts[1] = amounts[1] + unit * change
        amounts[2] = amounts[2] + change * change
        amounts[3] = amounts[3] + change * image
    scalar_ref[...] = lanes([total(amount) for amount in amounts], LANES)
    known_ref[...] = lanes([rayleigh, scale], LANES)


def ritz_kernel(
    place_ref, size_ref, gathered_ref, known_ref, sums_ref,
    diagonal_ref, rows_ref, image_ref, change_ref,
    vector_ref, residual_ref, energies_ref,
):
    change_energy, correlation, square, change_image = scalars_of(gathered_ref, 4)
    known = known_ref[...]
    rayleigh = widened(known, 0)
    scale = widened(known, 1)
    spread = square - correlation * correlation
    deviation = jnp.sqrt(spread)
    inverse = 1.0 / deviation
    shrink = 1.0 / scale
    cross_term = (change_image - correlation * rayleigh) * inverse
    second_energy = (
        change_energy - 2.0 * correlation * change_image + correlation * correlation * rayleigh
    ) / spread
    half_gap = 0.5 * (rayleigh - second_energy)
    length = jnp.sqrt(half_gap * half_gap + cross_term * cross_term)
    lowest = 0.5 * (rayleigh + second_energy) - length
    apart = length > 0.0
    divisor = jnp.where(apart, length, 1.0)
    double_cosine = jnp.where(apart, half_gap / divisor, 1.0)
    double_sine = jnp.where(apart, cross_term / divisor, 0.0)
    larger = jnp.sqrt(0.5 * (1.0 + jnp.abs(double_cosine)))
    smaller = 0.5 * double_sine / larger
    ahead = double_cosine >= 0.0
    sign = jnp.where(cross_term < 0.0, -1.0, 1.0)
    cosine_angle = jnp.where(ahead, larger, jnp.abs(smaller))
    sine_angle = jnp.where(ahead, smaller, sign * larger)
    first_row = own_rows(place_ref)
    for block in range(2):
        mask = inside(size_of(place_ref, size_ref, block), first_row, (ROWS, WIDTH))
        unit = rows_ref[block] * shrink
        image = image_ref[block]
        change = change_ref[block]
        rounded = change.astype(BF16).astype(F32)
        change_picture = jnp.where(mask, sums_ref[block] + diagonal_ref[block] * rounded, 0.0)
        unit_second = (change - correlation * unit) * inverse
        second_image = (change_picture - correlation * image) * inverse
        ritz_unit = sine_angle * unit - cosine_angle * unit_second
        vector_ref[block] = (scale * ritz_unit).astype(BF16)
        residual_ref[block] = (
            scale * (sine_angle * image - cosine_angle * second_image - lowest * ritz_unit)
        ).astype(BF16)
    energies_ref[...] = lanes([rayleigh, lowest], 2)


def body(start, left, right, left_energy, right_energy, sector_size, sector_spin):
    core = lax.axis_index("c")
    position = lax.axis_index(OP)
    sectors = lax.axis_size(SEC)
    place = jnp.stack([core, position, 2 * lax.axis_index(SEC)]).astype(jnp.int32)
    block_shape = shaped((WIDTH, WIDTH), BF16)
    two_shape = shaped((2, WIDTH, WIDTH), BF16)
    own_shape = shaped((2, ROWS, WIDTH), F32)
    lane_shape = shaped((1, LANES), F32)
    work = 8 * WIDTH * WIDTH * WIDTH
    owners = ("c",) + SEC
    within = [(i, sectors + i) for i in range(sectors)]
    across = [(sectors + i, i + 1) for i in range(sectors - 1)]
    to_next = within + across
    to_previous = [(there, here) for here, there in to_next]

    halo_source, send, own = call(
        open_kernel,
        (block_shape, two_shape, shaped((3, WIDTH, WIDTH), BF16)),
        [HBM] * 3,
        [pltpu.SemaphoreType.DMA((6,))],
        vmem=WHOLE_VMEM,
    )(start, left, right)
    other = lax.ppermute(send, "c", [(0, 1), (1, 0)])
    halo = lax.ppermute(halo_source, owners, [(there, here) for here, there in across])
    operators = (own, other)
    rows, diagonal, amounts = call(
        rows_kernel, (own_shape, own_shape, lane_shape), [SM] * 2 + [VM] * 3
    )(place, sector_size, start, left_energy, right_energy)

    def summed(lowered, raised, amounts):
        arrived = lax.ppermute(raised, owners, to_next)
        parts = call(parts_kernel, shaped((NOP, PART, LANES), BF16), [VM] * 3)(
            lowered, arrived, amounts
        )
        sums, scalars = call(sum_kernel, (own_shape, shaped((sectors, 1, LANES), F32)), [VM])(
            lax.all_to_all(parts, OP, 0, 0)
        )
        return sums, lax.all_to_all(scalars, SEC, 0, 0)

    lowered_shapes = (shaped((WIDTH, WIDTH), F32), lane_shape)
    raised = call(
        first_raise_kernel, block_shape, [SM] * 3 + [VM] * 2, flops=work, nbytes=4 << 20
    )(place, sector_size, sector_spin, *operators)
    lowered, amounts = call(
        first_lower_kernel, lowered_shapes, [SM] * 3 + [VM] * 6, flops=work, nbytes=4 << 20
    )(place, sector_size, sector_spin, start, halo, raised, amounts, *operators)
    sums, gathered = summed(lowered, raised, amounts)
    spread, image, change, amounts, known = call(
        correction_kernel,
        (shaped((NOP, ROWS, WIDTH), BF16), own_shape, own_shape, lane_shape, lane_shape),
        [SM] * 2 + [VM] * 4,
    )(place, sector_size, gathered, sums, diagonal, rows)
    field = lax.all_to_all(spread, OP, 0, 0)
    after = lax.ppermute(field, owners, to_previous)
    raised = call(
        second_raise_kernel, block_shape, [SM] * 2 + [VM] * 3, flops=work, nbytes=4 << 20
    )(place, sector_spin, field, *operators)
    lowered, amounts = call(
        second_lower_kernel, lowered_shapes, [SM] * 2 + [VM] * 5, flops=work, nbytes=4 << 20
    )(place, sector_spin, after, raised, amounts, *operators)
    sums, gathered = summed(lowered, raised, amounts)
    result = shaped((2, ROWS, WIDTH), BF16)
    vector, residual, energies = call(
        ritz_kernel, (result, result, shaped((1, 2), F32)), [SM] * 2 + [VM] * 7
    )(place, sector_size, gathered, known, sums, diagonal, rows, image, change)
    return vector, residual, energies.reshape(2)


def solution(mesh):
    fine = Mesh(mesh.devices.reshape(2, 4, 2, 2, 16), ("yh", "x", "c", "yl", "z"))
    return jax.shard_map(
        body,
        mesh=fine,
        in_specs=(
            P(SEC, None, None),
            P(OP, SEC, None, None),
            P(OP, SEC, None, None),
            P(SEC, None),
            P(SEC, None),
            P(),
            P(),
        ),
        out_specs=(P(SEC, OP, None), P(SEC, OP, None), P()),
        check_vma=False,
    )
```

```python
import jax
import jax.numpy as jnp
from jax import lax
from jax.experimental import pallas as pl
from jax.experimental.pallas import tpu as pltpu
from jax.sharding import Mesh, PartitionSpec as P

F32 = jnp.float32
BF16 = jnp.bfloat16
OP = ("yh", "x", "c")
SEC = ("yl", "z")
WIDTH = 512
ROWS = 32
NOP = 16
LANES = 128
TILES = WIDTH // LANES
PART = ROWS * TILES + 16
VMEM_LIMIT = 24 * 1024 * 1024
WHOLE_VMEM = 54 * 1024 * 1024

VM = pl.BlockSpec(memory_space=pltpu.VMEM)
SM = pl.BlockSpec(memory_space=pltpu.SMEM)
HBM = pl.BlockSpec(memory_space=pltpu.HBM)


def call(
    kernel, out_shape, in_specs, scratch=(), flops=0, nbytes=1 << 20, vmem=VMEM_LIMIT
):
    return pl.pallas_call(
        kernel,
        out_shape=out_shape,
        in_specs=in_specs,
        out_specs=jax.tree.map(lambda _: VM, out_shape),
        scratch_shapes=list(scratch),
        compiler_params=pltpu.CompilerParams(vmem_limit_bytes=vmem),
        cost_estimate=pl.CostEstimate(flops=flops, bytes_accessed=nbytes, transcendentals=0),
    )


def shaped(shape, dtype):
    return jax.ShapeDtypeStruct(shape, dtype)


def product(first, second, second_axis=0):
    return lax.dot_general(
        first, second, (((1,), (second_axis,)), ((), ())), preferred_element_type=F32
    )


def total(array):
    return jnp.sum(jnp.sum(array, axis=0, keepdims=True), axis=1, keepdims=True)


def lanes(values, width):
    place = lax.broadcasted_iota(jnp.int32, (1, width), 1)
    row = jnp.zeros((1, width), F32)
    for index, value in enumerate(values):
        row = jnp.where(place == index, value if value.shape[1] == 1 else value[:, :width], row)
    return row


def three_parts(row):
    high = row.astype(BF16).astype(F32)
    middle = (row - high).astype(BF16).astype(F32)
    return high, middle, (row - high) - middle


def stacked(rows, count, width):
    place = lax.broadcasted_iota(jnp.int32, (count, width), 0)
    block = jnp.zeros((count, width), F32)
    for index, row in enumerate(rows):
        block = jnp.where(place == index, row, block)
    return block.astype(BF16)


def own_rows(place_ref):
    return pl.multiple_of(place_ref[1] * ROWS, ROWS)


def inside(size, first_row, shape):
    rows = lax.broadcasted_iota(jnp.int32, shape, 0) + first_row
    columns = lax.broadcasted_iota(jnp.int32, shape, 1)
    return (rows < size) & (columns < size)


def size_of(place_ref, size_ref, block):
    return size_ref[jnp.minimum(place_ref[2] + block, size_ref.shape[0] - 1)]


def diagonal_of(left_row, right_row, first_row):
    rows = lax.broadcasted_iota(jnp.int32, (ROWS, WIDTH), 0) + first_row
    columns = lax.broadcasted_iota(jnp.int32, (ROWS, WIDTH), 1)
    chosen = jnp.where(rows == columns, left_row, 0.0)
    return jnp.sum(chosen, axis=1, keepdims=True) + right_row


def open_kernel(start_ref, left_ref, right_ref, halo_ref, send_ref, own_ref, semaphores):
    core = lax.axis_index("c")
    copies = [
        pltpu.make_async_copy(source, target, semaphores.at[index])
        for index, (source, target) in enumerate(
            (
                (left_ref.at[0, 1 - core], send_ref.at[0]),
                (right_ref.at[0, 1 - core], send_ref.at[1]),
                (start_ref.at[0], halo_ref),
                (left_ref.at[0, core], own_ref.at[0]),
                (right_ref.at[0, core], own_ref.at[1]),
                (start_ref.at[core], own_ref.at[2]),
            )
        )
    ]
    for copy in copies:
        copy.start()
    for copy in copies:
        copy.wait()


def rows_kernel(
    place_ref, size_ref, start_ref, left_levels_ref, right_levels_ref,
    rows_ref, diagonal_ref, scalar_ref,
):
    first_row = own_rows(place_ref)
    norm = jnp.zeros((ROWS, WIDTH), F32)
    energy = jnp.zeros((ROWS, WIDTH), F32)
    for block in range(2):
        mask = inside(size_of(place_ref, size_ref, block), first_row, (ROWS, WIDTH))
        own = jnp.where(mask, start_ref[block, pl.ds(first_row, ROWS)].astype(F32), 0.0)
        rows_ref[block] = own
        square = own * own
        norm = norm + square
        diagonal = diagonal_of(
            left_levels_ref[block : block + 1], right_levels_ref[block : block + 1], first_row
        )
        diagonal_ref[block] = diagonal
        energy = energy + diagonal * square
    scalar_ref[...] = lanes([total(energy), total(norm)], LANES)


def masked(source, place_ref, size_ref, block):
    mask = inside(size_of(place_ref, size_ref, block), 0, (WIDTH, WIDTH))
    return jnp.where(mask, source.astype(F32), 0.0).astype(BF16)


def coupling_of(place_ref, spin_ref):
    here = place_ref[2] + place_ref[0]
    following = jnp.minimum(here + 1, spin_ref.shape[0] - 1)
    above = jnp.full((1, WIDTH), spin_ref[following], jnp.int32).astype(F32) + 1.0
    below = jnp.full((1, WIDTH), spin_ref[here], jnp.int32).astype(F32) + 1.0
    linked = jnp.full((1, WIDTH), here, jnp.int32) + 1 < spin_ref.shape[0]
    return jnp.where(linked, jnp.sqrt(above / below), 0.0)


def operator_pairs(own_ref, other_ref):
    return (own_ref[0], own_ref[1]), (other_ref[0], other_ref[1])


def raise_into(place_ref, spin_ref, own_ref, other_ref, field, raised_ref):
    image = jnp.zeros((WIDTH, WIDTH), F32)
    for left, right in operator_pairs(own_ref, other_ref):
        image = image + product(left, product(field, right, 1).astype(BF16))
    raised_ref[...] = (coupling_of(place_ref, spin_ref) * image).astype(BF16)


def lower_into(
    place_ref, spin_ref, own_ref, other_ref, after, raised_ref, scalars,
    lowered_ref, scalar_ref,
):
    image = jnp.zeros((WIDTH, WIDTH), F32)
    for left, right in operator_pairs(own_ref, other_ref):
        image = image + product(product(left.T, after).astype(BF16), right)
    lowered_ref[...] = coupling_of(place_ref, spin_ref) * image
    energy = 2.0 * total(raised_ref[...].astype(F32) * after.astype(F32))
    scalar_ref[...] = lanes([energy], LANES) + scalars


def first_raise_kernel(
    place_ref, size_ref, spin_ref, own_ref, other_ref, raised_ref
):
    core = place_ref[0]
    field = masked(own_ref[2], place_ref, size_ref, core)
    raise_into(place_ref, spin_ref, own_ref, other_ref, field, raised_ref)


def first_lower_kernel(
    place_ref, size_ref, spin_ref, start_ref, halo_ref, raised_ref, known_ref,
    own_ref, other_ref, lowered_ref, scalar_ref,
):
    core = place_ref[0]
    source = jnp.where(core == 0, start_ref[1].astype(F32), halo_ref[...].astype(F32))
    after = masked(source, place_ref, size_ref, core + 1)
    lower_into(
        place_ref, spin_ref, own_ref, other_ref, after, raised_ref, known_ref[...],
        lowered_ref, scalar_ref,
    )


def second_raise_kernel(
    place_ref, spin_ref, gathered_ref, own_ref, other_ref, raised_ref
):
    field = gathered_ref[...].reshape(WIDTH, WIDTH)
    raise_into(place_ref, spin_ref, own_ref, other_ref, field, raised_ref)


def second_lower_kernel(
    place_ref, spin_ref, after_ref, raised_ref, known_ref, own_ref, other_ref,
    lowered_ref, scalar_ref,
):
    after = after_ref[...].reshape(WIDTH, WIDTH)
    lower_into(
        place_ref, spin_ref, own_ref, other_ref, after, raised_ref, known_ref[...],
        lowered_ref, scalar_ref,
    )


def parts_kernel(lowered_ref, arrived_ref, scalar_ref, parts_ref):
    coded = stacked(three_parts(scalar_ref[...]), 16, LANES)
    for device in range(NOP):
        here = slice(device * ROWS, (device + 1) * ROWS)
        image = (lowered_ref[here] + arrived_ref[here].astype(F32)).astype(BF16)
        for tile in range(TILES):
            columns = slice(tile * LANES, (tile + 1) * LANES)
            parts_ref[device, tile * ROWS : (tile + 1) * ROWS] = image[:, columns]
        parts_ref[device, ROWS * TILES :] = coded


def sum_kernel(received_ref, sums_ref, scalar_ref):
    coded = jnp.zeros((16, LANES), F32)
    for device in range(NOP):
        coded = coded + received_ref[device, ROWS * TILES :].astype(F32)
    row = jnp.sum(coded, axis=0, keepdims=True)
    scalar_ref[...] = jnp.broadcast_to(row[None], scalar_ref.shape)
    for block in range(2):
        for tile in range(TILES):
            running = jnp.zeros((ROWS, LANES), F32)
            for device in range(block, NOP, 2):
                here = slice(tile * ROWS, (tile + 1) * ROWS)
                running = running + received_ref[device, here].astype(F32)
            sums_ref[block, :, tile * LANES : (tile + 1) * LANES] = running


def widened(row, index):
    return jnp.broadcast_to(row[:, index : index + 1], (1, WIDTH))


def scalars_of(gathered_ref, count):
    row = jnp.sum(gathered_ref[...], axis=0)
    return [widened(row, index) for index in range(count)]


def correction_kernel(
    place_ref, size_ref, gathered_ref, sums_ref, diagonal_ref, rows_ref,
    spread_ref, image_ref, change_ref, scalar_ref, known_ref,
):
    energy, norm = scalars_of(gathered_ref, 2)
    rayleigh = energy / norm
    scale = jnp.sqrt(norm)
    shrink = 1.0 / scale
    first_row = own_rows(place_ref)
    amounts = [jnp.zeros((ROWS, WIDTH), F32) for _ in range(4)]
    for block in range(2):
        mask = inside(size_of(place_ref, size_ref, block), first_row, (ROWS, WIDTH))
        values = rows_ref[block]
        diagonal = diagonal_ref[block]
        unit = values * shrink
        image = jnp.where(mask, sums_ref[block] + diagonal * values, 0.0) * shrink
        residual = image - rayleigh * unit
        change = residual / (jnp.abs(diagonal - rayleigh) + 1.0)
        rounded = change.astype(BF16)
        for device in range(block, NOP, 2):
            spread_ref[device] = rounded
        image_ref[block] = image
        change_ref[block] = change
        again = rounded.astype(F32)
        amounts[0] = amounts[0] + diagonal * again * again
        amounts[1] = amounts[1] + unit * change
        amounts[2] = amounts[2] + change * change
        amounts[3] = amounts[3] + change * image
    scalar_ref[...] = lanes([total(amount) for amount in amounts], LANES)
    known_ref[...] = lanes([rayleigh, scale], LANES)


def ritz_kernel(
    place_ref, size_ref, gathered_ref, known_ref, sums_ref,
    diagonal_ref, rows_ref, image_ref, change_ref,
    vector_ref, residual_ref, energies_ref,
):
    change_energy, correlation, square, change_image = scalars_of(gathered_ref, 4)
    known = known_ref[...]
    rayleigh = widened(known, 0)
    scale = widened(known, 1)
    spread = square - correlation * correlation
    deviation = jnp.sqrt(spread)
    inverse = 1.0 / deviation
    shrink = 1.0 / scale
    cross_term = (change_image - correlation * rayleigh) * inverse
    second_energy = (
        change_energy - 2.0 * correlation * change_image + correlation * correlation * rayleigh
    ) / spread
    half_gap = 0.5 * (rayleigh - second_energy)
    length = jnp.sqrt(half_gap * half_gap + cross_term * cross_term)
    lowest = 0.5 * (rayleigh + second_energy) - length
    apart = length > 0.0
    divisor = jnp.where(apart, length, 1.0)
    double_cosine = jnp.where(apart, half_gap / divisor, 1.0)
    double_sine = jnp.where(apart, cross_term / divisor, 0.0)
    larger = jnp.sqrt(0.5 * (1.0 + jnp.abs(double_cosine)))
    smaller = 0.5 * double_sine / larger
    ahead = double_cosine >= 0.0
    sign = jnp.where(cross_term < 0.0, -1.0, 1.0)
    cosine_angle = jnp.where(ahead, larger, jnp.abs(smaller))
    sine_angle = jnp.where(ahead, smaller, sign * larger)
    first_row = own_rows(place_ref)
    for block in range(2):
        mask = inside(size_of(place_ref, size_ref, block), first_row, (ROWS, WIDTH))
        unit = rows_ref[block] * shrink
        image = image_ref[block]
        change = change_ref[block]
        rounded = change.astype(BF16).astype(F32)
        change_picture = jnp.where(mask, sums_ref[block] + diagonal_ref[block] * rounded, 0.0)
        unit_second = (change - correlation * unit) * inverse
        second_image = (change_picture - correlation * image) * inverse
        ritz_unit = sine_angle * unit - cosine_angle * unit_second
        vector_ref[block] = (scale * ritz_unit).astype(BF16)
        residual_ref[block] = (
            scale * (sine_angle * image - cosine_angle * second_image - lowest * ritz_unit)
        ).astype(BF16)
    energies_ref[...] = lanes([rayleigh, lowest], 2)


def body(start, left, right, left_energy, right_energy, sector_size, sector_spin):
    core = lax.axis_index("c")
    position = lax.axis_index(OP)
    sectors = lax.axis_size(SEC)
    place = jnp.stack([core, position, 2 * lax.axis_index(SEC)]).astype(jnp.int32)
    block_shape = shaped((WIDTH, WIDTH), BF16)
    two_shape = shaped((2, WIDTH, WIDTH), BF16)
    own_shape = shaped((2, ROWS, WIDTH), F32)
    lane_shape = shaped((1, LANES), F32)
    work = 8 * WIDTH * WIDTH * WIDTH
    owners = ("c",) + SEC
    within = [(i, sectors + i) for i in range(sectors)]
    across = [(sectors + i, i + 1) for i in range(sectors - 1)]
    to_next = within + across
    to_previous = [(there, here) for here, there in to_next]

    halo_source, send, own = call(
        open_kernel,
        (block_shape, two_shape, pltpu.VMEM((3, WIDTH, WIDTH), BF16)),
        [HBM] * 3,
        [pltpu.SemaphoreType.DMA((6,))],
        vmem=WHOLE_VMEM,
    )(start, left, right)
    other = lax.ppermute(send, "c", [(0, 1), (1, 0)])
    halo = lax.ppermute(halo_source, owners, [(there, here) for here, there in across])
    operators = (own, other)
    rows, diagonal, amounts = call(
        rows_kernel, (own_shape, own_shape, lane_shape), [SM] * 2 + [VM] * 3
    )(place, sector_size, start, left_energy, right_energy)

    def summed(lowered, raised, amounts):
        arrived = lax.ppermute(raised, owners, to_next)
        parts = call(parts_kernel, shaped((NOP, PART, LANES), BF16), [VM] * 3)(
            lowered, arrived, amounts
        )
        sums, scalars = call(sum_kernel, (own_shape, shaped((sectors, 1, LANES), F32)), [VM])(
            lax.all_to_all(parts, OP, 0, 0)
        )
        return sums, lax.all_to_all(scalars, SEC, 0, 0)

    lowered_shapes = (shaped((WIDTH, WIDTH), F32), lane_shape)
    raised = call(
        first_raise_kernel, block_shape, [SM] * 3 + [VM] * 2, flops=work, nbytes=4 << 20
    )(place, sector_size, sector_spin, *operators)
    lowered, amounts = call(
        first_lower_kernel, lowered_shapes, [SM] * 3 + [VM] * 6, flops=work, nbytes=4 << 20
    )(place, sector_size, sector_spin, start, halo, raised, amounts, *operators)
    sums, gathered = summed(lowered, raised, amounts)
    spread, image, change, amounts, known = call(
        correction_kernel,
        (shaped((NOP, ROWS, WIDTH), BF16), own_shape, own_shape, lane_shape, lane_shape),
        [SM] * 2 + [VM] * 4,
    )(place, sector_size, gathered, sums, diagonal, rows)
    field = lax.all_to_all(spread, OP, 0, 0)
    after = lax.ppermute(field, owners, to_previous)
    raised = call(
        second_raise_kernel, block_shape, [SM] * 2 + [VM] * 3, flops=work, nbytes=4 << 20
    )(place, sector_spin, field, *operators)
    lowered, amounts = call(
        second_lower_kernel, lowered_shapes, [SM] * 2 + [VM] * 5, flops=work, nbytes=4 << 20
    )(place, sector_spin, after, raised, amounts, *operators)
    sums, gathered = summed(lowered, raised, amounts)
    result = shaped((2, ROWS, WIDTH), BF16)
    vector, residual, energies = call(
        ritz_kernel, (result, result, shaped((1, 2), F32)), [SM] * 2 + [VM] * 7
    )(place, sector_size, gathered, known, sums, diagonal, rows, image, change)
    return vector, residual, energies.reshape(2)


def solution(mesh):
    fine = Mesh(mesh.devices.reshape(2, 4, 2, 2, 16), ("yh", "x", "c", "yl", "z"))
    return jax.shard_map(
        body,
        mesh=fine,
        in_specs=(
            P(SEC, None, None),
            P(OP, SEC, None, None),
            P(OP, SEC, None, None),
            P(SEC, None),
            P(SEC, None),
            P(),
            P(),
        ),
        out_specs=(P(SEC, OP, None), P(SEC, OP, None), P()),
        check_vma=False,
    )
```
